32 devices in a mesh: side: 2 (over core), grp: 4 (over y, x), tp: 4 (over z).
Axes of the slice: x: 2, y: 2, z: 4, core: 2. Of those that a mesh axis runs over, the one named last changes fastest.
Arguments:
- queries: bfloat16 [96, 4096], P('grp', 'side'), may hold values from -6 to 6
- kv_cache: bfloat16 [96, 8, 384, 256], P('grp', ('side', 'tp')), may hold values from -6 to 6
- lengths: int32 [96], P('grp'), may hold values from 2 to 768, as said below
- out_weight: bfloat16 [4096, 2048], P(('side', 'tp')), may hold values from -1 to 1
- resid: bfloat16 [96, 2048], P('grp'), may hold values from -6 to 6
- norm_gain: float32 [2048], replicated, may hold values from 0.1 to 1.9
- expert_ids: int32 [96, 8], P('grp'), may hold values from 0 to 31, all different within a row; in each aligned block of 24 rows (0 to 23, 24 to 47, ...) at most 12 rows name the same one
- expert_gates: float32 [96, 8], P('grp'), may hold values from 0.05 to 1
- w_gate_up: bfloat16 [32, 2048, 1536], P(('side', 'grp', 'tp')), may hold values from -0.125 to 0.125
- w_down: bfloat16 [32, 768, 2048], P(('side', 'grp', 'tp')), may hold values from -0.21875 to 0.21875
Outputs:
- layer_out: bfloat16 [96, 2048], P('grp', ('side', 'tp'))
The draws below stay inside these ranges and needn't reach their ends.
Inputs may be any that keep to these rules, and one draw needn't show every extreme that they name: `lengths`: every row's cache holds at least two tokens; some row holds exactly 768. `expert_ids`: each row names 8 different experts. Among the rows of one row group no expert is named by more than 12 rows; in some group an expert is named by exactly 12.
All inputs are finite; a program needn't handle non-finite values.
Results may differ from the reference program's by a relative error of at most 0.017.
Values may be sent and summed in bfloat16 or wider, within the bound.
No kernel may reach another device: no remote copies, remote signals or barrier semaphores. Data moves between devices by JAX's collectives and lax.ppermute only.
A program may use at most 64 MiB of HBM per device.

```python
import math
import jax
import jax.numpy as jnp
import numpy as np
from jax import lax

D = 2048
QH = 32
KVH = 4
HD = 128
FFE = 768
TOPK = 8
L = 768
ROWS_GRP = 24
EXPERTS = 32
ROWS = 96
KV_PARTS = 2
L_PART = 384
CAP = 12
N_GRP = 4


def draw_queries(key, part):
    drawn = jnp.clip(jax.random.normal(jax.random.fold_in(key, 11), (ROWS, QH, HD), jnp.float32), -6.0, 6.0)
    return drawn.reshape(ROWS, QH * HD).astype(jnp.bfloat16)


def draw_kv_cache(key, part):
    drawn = jnp.clip(jax.random.normal(jax.random.fold_in(key, 12), (ROWS, KVH * KV_PARTS, L_PART, 2 * HD), jnp.float32), -6.0, 6.0)
    return drawn.astype(jnp.bfloat16)


def draw_lengths(key, part):
    drawn_lengths = jax.random.randint(jax.random.fold_in(key, 13), (ROWS,), 2, L + 1)
    full_row = jax.random.randint(jax.random.fold_in(key, 14), (), 0, ROWS)
    return jnp.where(jnp.arange(ROWS) == full_row, L, drawn_lengths).astype(jnp.int32)


def level_of(stream_key, extent, shards, smallest, high):
    def one(position, blocks):
        heights = jax.random.uniform(jax.random.fold_in(jax.random.fold_in(stream_key, 6), position), (blocks,), jnp.float32, smallest / len(shards), high / len(shards))
        return jnp.repeat(jnp.exp(heights), extent[position] // blocks).reshape((-1,) + (1,) * (len(extent) - position - 1))

    factor_of = one(*shards[0])
    for cut in shards[1:]:
        factor_of = factor_of * one(*cut)
    return factor_of


def assign_block(stream_key, own, number, rows, number_of, top, limit, slope):
    order = jax.random.permutation(stream_key, number_of)
    crowded, usual = shares(number_of, rows * top, limit, slope, True), shares(number_of, rows * top, limit, slope, False)
    places = jnp.arange(number_of)

    def named(sizes, rotation):
        used = int((sizes > 0).sum())
        fixed = max(1, used // 4)
        shifted = fixed + (places - fixed + rotation * (used - fixed)) % max(1, number_of - fixed)
        return jnp.zeros((number_of,), jnp.int32).at[order[jnp.where(places < fixed, places, shifted)]].set(jnp.asarray(sizes, jnp.int32))

    sizes = jnp.where(number % 4 == 0, named(crowded, number // 4), named(usual, number - number // 4 - 1))
    mixed = jax.random.permutation(jax.random.fold_in(own, 3), number_of)
    source_of, taker = mixed[0:number_of // 2 * 2:2], mixed[1:number_of // 2 * 2:2]
    slack = jnp.minimum(sizes[source_of] - 1, limit - sizes[taker]) // 2
    slack = jnp.where((source_of == order[0]) | (taker == order[0]) | (sizes[taker] == 0), 0, jnp.maximum(slack, 0))
    shifted = jax.random.randint(jax.random.fold_in(own, 4), (number_of // 2,), 0, 1 << 20) % (slack + 1)
    sizes = sizes.at[source_of].add(-shifted).at[taker].add(shifted)
    members = jnp.searchsorted(jnp.cumsum(sizes), jnp.arange(rows * top), side="right").astype(jnp.int32)
    listing = members.reshape(top, rows).T
    listing = listing[jax.random.permutation(jax.random.fold_in(own, 1), rows)]
    rotation = jax.random.randint(jax.random.fold_in(own, 2), (rows, 1), 0, top)
    return jnp.take_along_axis(listing, (jnp.arange(top)[None, :] + rotation) % top, axis=1)


def shares(number_of, total, limit, slope, full):
    loads = [(1 << 20) // math.isqrt(standing ** slope) + 1 for standing in range(1, number_of + 1)]
    largest = limit if full else min(limit, max(-(-total // number_of), total * loads[0] // sum(loads)))
    least = 1 if total - largest >= number_of - 1 else 0
    holding, spare = [largest] + [least] * (number_of - 1), total - largest - least * (number_of - 1)
    while spare > 0:
        movable = [i for i in range(1, number_of) if holding[i] < largest] or [i for i in range(1, number_of) if holding[i] < limit]
        mass, left = sum([loads[i] for i in movable]), spare
        for i in movable:
            more = min(limit - holding[i], max(1, left * loads[i] // mass), spare)
            holding[i] = holding[i] + more
            spare = spare - more
    return np.array(holding)


def gaussian(stream_key, dims, width, most, pieces=(), kind=jnp.bfloat16):
    values = jax.random.normal(stream_key, dims, jnp.float32) * width
    if len(pieces) > 0:
        values = level_of(stream_key, dims, pieces, -0.22, 0.18) * values
    return jnp.clip(values, min=-most, max=most).astype(kind)


def setup_inputs(seed: int = 0) -> dict:
    arg_keys = jax.random.split(jax.random.key(seed), 11)
    queries = draw_queries(jax.random.fold_in(arg_keys[10], 71), 0)
    kv_cache = draw_kv_cache(jax.random.fold_in(arg_keys[10], 71), 0)
    lengths = draw_lengths(jax.random.fold_in(arg_keys[10], 71), 0)
    out_weight = gaussian(arg_keys[3], (QH * HD, D), QH ** -0.5, 1.0, ((0, 8),))
    resid = gaussian(arg_keys[4], (ROWS, D), 1.0, 6.0, ((0, 4),))
    norm_gain = jnp.clip(1.0 + 0.18 * jax.random.normal(arg_keys[5], (D,), jnp.float32), 0.1, 1.9)
    expert_ids_keys = jax.random.split(jax.random.fold_in(arg_keys[6], 1), ROWS // ROWS_GRP)
    expert_ids_turns = jax.random.permutation(jax.random.fold_in(arg_keys[6], 3), ROWS // ROWS_GRP)
    expert_ids = jax.vmap(lambda own, number: assign_block(jax.random.fold_in(arg_keys[6], 2), own, number, ROWS_GRP, EXPERTS, TOPK, CAP, 2))(expert_ids_keys, expert_ids_turns).reshape((ROWS, TOPK))
    expert_gates = jnp.clip(jnp.exp(math.log(1.0) - 2.9957323 * jax.random.uniform(arg_keys[7], (ROWS, TOPK), jnp.float32) ** level_of(arg_keys[7], (ROWS, TOPK), ((0, 4),), -0.2, 0.2)), 0.05, 1.0)
    w_gate_up = gaussian(arg_keys[8], (EXPERTS, D, 2 * FFE), D ** -0.5, 0.125, ((0, 32),))
    w_down = gaussian(arg_keys[9], (EXPERTS, FFE, D), FFE ** -0.5, 0.21875, ((0, 32),))
    return {"queries": queries, "kv_cache": kv_cache, "lengths": lengths, "out_weight": out_weight, "resid": resid, "norm_gain": norm_gain, "expert_ids": expert_ids, "expert_gates": expert_gates, "w_gate_up": w_gate_up, "w_down": w_down}


def reference(queries, kv_cache, lengths, out_weight, resid, norm_gain, expert_ids, expert_gates, w_gate_up, w_down):
    row_total = queries.shape[0]
    group_heads = QH // KVH
    kv_whole = kv_cache.reshape(row_total, KVH, KV_PARTS * L_PART, 2 * HD)
    key_rows = kv_whole[..., :HD].astype(jnp.float32)
    value_rows = kv_whole[..., HD:].astype(jnp.float32)
    query_rows = queries.reshape(row_total, KVH, group_heads, HD).astype(jnp.float32)
    scores = jnp.einsum('rhgd,rhpd->rhgp', query_rows, key_rows) / math.sqrt(HD)
    valid_mask = (jnp.arange(KV_PARTS * L_PART, dtype=jnp.int32)[None, :] < lengths[:, None])[:, None, None, :]
    masked = jnp.where(valid_mask, scores, -1e+30)
    row_max = lax.optimization_barrier(jnp.max(masked, axis=-1, keepdims=True))
    weights = jnp.where(valid_mask, jnp.exp(masked - row_max), 0.0)
    weight_sum = lax.optimization_barrier(jnp.sum(weights, axis=-1))
    probs = lax.optimization_barrier(weights.astype(jnp.bfloat16))
    numerator = jnp.einsum('rhgp,rhpd->rhgd', probs.astype(jnp.float32), value_rows)
    heads_out = (numerator / weight_sum[..., None]).astype(jnp.bfloat16).reshape(row_total, QH * HD)
    projected = jnp.dot(heads_out, out_weight, preferred_element_type=jnp.float32)
    middle = (resid.astype(jnp.float32) + projected).astype(jnp.bfloat16)
    middle_wide = middle.astype(jnp.float32)
    inv_rms = lax.rsqrt(lax.optimization_barrier(jnp.mean(middle_wide * middle_wide, axis=-1, keepdims=True)) + 1e-06)
    normed = (middle_wide * inv_rms * norm_gain).astype(jnp.bfloat16)
    experts = w_gate_up.shape[0]
    matches = expert_ids[:, :, None] == jnp.arange(experts, dtype=jnp.int32)[None, None, :]
    coefficients = lax.optimization_barrier(jnp.sum(jnp.where(matches, expert_gates[:, :, None], 0.0), axis=1))
    routed = jnp.any(matches, axis=1).astype(jnp.int32)
    most_rows = N_GRP * CAP

    def one_expert(accumulated, expert_index):
        flags = jnp.take(routed, expert_index, axis=1)
        row_order = jnp.argsort(1 - flags, stable=True)[:most_rows].astype(jnp.int32)
        picked = normed[row_order]
        hidden = jnp.dot(picked, w_gate_up[expert_index], preferred_element_type=jnp.float32)
        activated = (jax.nn.silu(hidden[:, :FFE]) * hidden[:, FFE:]).astype(jnp.bfloat16)
        result = jnp.dot(activated, w_down[expert_index], preferred_element_type=jnp.float32).astype(jnp.bfloat16)
        weighted = coefficients[row_order, expert_index][:, None] * result.astype(jnp.float32)
        return (accumulated.at[row_order].add(weighted), None)
    moe, _ = lax.scan(one_expert, jnp.zeros((row_total, D), jnp.float32), jnp.arange(experts, dtype=jnp.int32))
    return (middle_wide + moe).astype(jnp.bfloat16)
```

```python
import math

import jax
import jax.numpy as jnp
from jax import lax
from jax.sharding import PartitionSpec as P

QH = 32
KVH = 4
HD = 128


def swapped(value, axis, mask):
    pairs = [(source, source ^ mask) for source in range(lax.axis_size(axis))]
    return lax.ppermute(value, axis, pairs)


def body(
    queries,
    kv_cache,
    lengths,
    out_weight,
    resid,
    norm_gain,
    expert_ids,
    expert_gates,
    w_gate_up,
    w_down,
):
    f32, bf16 = jnp.float32, jnp.bfloat16
    tp = lax.axis_size("tp")
    grp = lax.axis_size("grp")
    sides = lax.axis_size("side")
    tp_index = lax.axis_index("tp")
    grp_index = lax.axis_index("grp")
    section = lax.axis_index("side")
    group_size = sides * tp
    kv_parts = group_size // KVH
    group_heads = QH // KVH
    per_member = QH // group_size
    part_span = kv_cache.shape[2]
    model_width = out_weight.shape[1]
    half = model_width // sides
    piece = model_width // group_size
    rows = lengths.shape[0]
    part_index = tp_index % kv_parts
    head_start = tp_index // kv_parts * group_heads * HD
    query_rows = lax.dynamic_slice_in_dim(queries, head_start, group_heads * HD, 1).reshape(
        rows, group_heads, HD
    )
    key_rows = kv_cache[:, 0, :, :HD]
    value_rows = kv_cache[:, 0, :, HD:]
    positions = part_index * part_span + jnp.arange(part_span, dtype=jnp.int32)
    valid_mask = (positions[None, :] < lengths[:, None])[:, None, :]
    scores = jnp.einsum(
        "rgd,rpd->rgp", query_rows, key_rows, preferred_element_type=f32
    ) / math.sqrt(HD)
    scores = jnp.where(valid_mask, scores, -1e30)
    row_max = jnp.max(scores, axis=-1)
    weights = jnp.where(valid_mask, jnp.exp(scores - row_max[..., None]), 0.0)
    weight_sum = jnp.sum(weights, axis=-1)
    numerator = jnp.einsum(
        "rgp,rpd->rgd", weights.astype(bf16), value_rows, preferred_element_type=f32
    )
    stats = jnp.stack([row_max, weight_sum], -1)
    packed = jnp.concatenate(
        [numerator, jnp.pad(stats, ((0, 0), (0, 0), (0, HD - 2)))], -1
    )

    def chunk_of(part):
        return lax.dynamic_slice_in_dim(packed, part * per_member, per_member, 1)

    parts = [chunk_of(part_index)]
    for mask in range(1, kv_parts):
        parts.append(swapped(chunk_of(part_index ^ mask), "tp", mask))
    whole_max = parts[0][..., HD]
    for part in parts[1:]:
        whole_max = jnp.maximum(whole_max, part[..., HD])
    total, total_sum = 0.0, 0.0
    for part in parts:
        factor = jnp.exp(part[..., HD] - whole_max)
        total = total + part[..., :HD] * factor[..., None]
        total_sum = total_sum + part[..., HD + 1] * factor
    mine = (total / total_sum[..., None]).astype(bf16).reshape(rows, per_member * HD)
    projected = jnp.dot(mine, out_weight, preferred_element_type=f32)
    away = lax.dynamic_slice_in_dim(projected, (1 - section) * half, half, 1).astype(bf16)
    kept = lax.dynamic_slice_in_dim(projected, section * half, half, 1)
    kept = kept + swapped(away, "side", 1).astype(f32)
    outgoing = kept.astype(bf16)
    arrived = [swapped(outgoing, "tp", mask) for mask in range(1, tp)]
    for other in arrived:
        kept = kept + other.astype(f32)
    resid_half = lax.dynamic_slice_in_dim(resid, section * half, half, 1)
    middle = (resid_half.astype(f32) + kept).astype(bf16)
    experts_all = sides * grp * tp
    dest = (section * grp + jnp.arange(grp, dtype=jnp.int32)) * tp + tp_index
    gate_cols = []
    for s in range(sides):
        dest = (s * grp + jnp.arange(grp, dtype=jnp.int32)) * tp + tp_index
        matches = expert_ids[:, :, None] == dest[None, None, :]
        gate_cols.append(jnp.sum(jnp.where(matches, expert_gates[:, :, None], 0.0), axis=1))
    my_gates = jnp.where(section == 0, gate_cols[0], gate_cols[1])
    gates_hi = my_gates.astype(bf16)
    gates_lo = (my_gates - gates_hi.astype(f32)).astype(bf16)
    gate_pairs = jnp.stack([gates_hi, gates_lo], -1)

    def packet(target):
        pair = lax.dynamic_index_in_dim(gate_pairs, target, 1, keepdims=False)
        return jnp.concatenate([middle, jnp.pad(pair, ((0, 0), (0, HD - 2)))], -1)

    groups = [packet(grp_index)]
    for mask in range(1, grp):
        groups.append(swapped(packet(grp_index ^ mask), "grp", mask))
    gathered = jnp.concatenate(groups, 0)
    own_half = gathered[:, :half]
    gate = gathered[:, half].astype(f32) + gathered[:, half + 1].astype(f32)
    other_half = swapped(own_half, "side", 1)
    left = jnp.where(section == 0, own_half, other_half)
    right = jnp.where(section == 0, other_half, own_half)
    rows_all = jnp.concatenate([left, right], 1).astype(f32)
    inv_rms = lax.rsqrt(jnp.mean(rows_all * rows_all, axis=-1, keepdims=True) + 1e-06)
    normed = (rows_all * inv_rms * norm_gain).astype(bf16)
    hidden = jnp.dot(normed, w_gate_up[0], preferred_element_type=f32)
    inner = hidden.shape[-1] // 2
    act = (jax.nn.silu(hidden[:, :inner]) * hidden[:, inner:]).astype(bf16)
    produced = jnp.dot(act, w_down[0], preferred_element_type=f32) * gate[:, None]
    sent = lax.dynamic_slice_in_dim(produced, (1 - section) * half, half, 1).astype(bf16)
    mine_out = lax.dynamic_slice_in_dim(produced, section * half, half, 1)
    mine_out = mine_out + swapped(sent, "side", 1).astype(f32)
    blocks = mine_out.reshape(grp, rows, half)
    back = blocks[0]
    for mask in range(1, grp):
        back = back + swapped(blocks[mask].astype(bf16), "grp", mask).astype(f32)

    def columns(index):
        return lax.dynamic_slice_in_dim(back, index * piece, piece, 1)

    final = lax.dynamic_slice_in_dim(middle, tp_index * piece, piece, 1).astype(f32)
    final = final + columns(tp_index)
    for mask in range(1, tp):
        final = final + swapped(columns(tp_index ^ mask).astype(bf16), "tp", mask).astype(f32)
    return final.astype(bf16)


def solution(mesh):
    in_specs = (
        P("grp", "side"),
        P("grp", ("side", "tp"), None, None),
        P("grp"),
        P(("side", "tp"), None),
        P("grp", None),
        P(),
        P("grp", None),
        P("grp", None),
        P(("side", "grp", "tp"), None, None),
        P(("side", "grp", "tp"), None, None),
    )
    out_specs = P("grp", ("side", "tp"))
    return jax.shard_map(body, mesh=mesh, in_specs=in_specs, out_specs=out_specs, check_vma=False)
```

```python
import functools
import math

import jax
import jax.numpy as jnp
from jax import lax
from jax.experimental import pallas as pl
from jax.experimental.pallas import tpu as pltpu
from jax.sharding import PartitionSpec as P

QH = 32
KVH = 4
HD = 128
LOW = -1e30
F32 = jnp.float32
BF16 = jnp.bfloat16
MIB = 1024 * 1024
VMEM_SPEC = pl.BlockSpec(memory_space=pltpu.VMEM)


def swapped(value, axis, mask):
    pairs = [(source, source ^ mask) for source in range(lax.axis_size(axis))]
    return lax.ppermute(value, axis, pairs)


def crossed(value, mask):
    grp, tp = lax.axis_size("grp"), lax.axis_size("tp")
    pairs = [
        ((s * grp + g) * tp + t, ((1 - s) * grp + (g ^ mask)) * tp + t)
        for s in range(2)
        for g in range(grp)
        for t in range(tp)
    ]
    return lax.ppermute(value, ("side", "grp", "tp"), pairs)


def near(value, space=pltpu.VMEM):
    return pltpu.with_memory_space_constraint(value, space)


def call(kernel, ins, outs, scratch=(), far=(), limit=8, name=None, cost=None):
    spaces = [pltpu.HBM if i in far else pltpu.VMEM for i in range(len(ins))]
    return pl.pallas_call(
        kernel,
        out_shape=[pltpu.VMEM(shape, dtype) for shape, dtype in outs],
        in_specs=[pl.BlockSpec(memory_space=s) for s in spaces],
        out_specs=[VMEM_SPEC] * len(outs),
        scratch_shapes=list(scratch),
        compiler_params=pltpu.CompilerParams(vmem_limit_bytes=limit * MIB),
        name=name,
        cost_estimate=cost,
    )(*[near(a, s) for a, s in zip(ins, spaces)])


def attention_kernel(sizes, *refs):
    tp, grp, sides, kv_parts, group_heads, per_member, rows, span, top, half = sizes
    q_hbm, len_hbm, ids_hbm, gates_hbm, kv_hbm, out_w_hbm, resid_hbm, gain_hbm = refs[:8]
    own_ref, *send_refs = refs[8 : 8 + kv_parts]
    lanes_ref, out_w_ref, resid_ref, gain_ref = refs[8 + kv_parts : 12 + kv_parts]
    kv, q_in, len_ref, ids_ref, gates_ref, turn_s, q_s, score_s, num_s, max_s, sum_s, sems = refs[
        12 + kv_parts :
    ]
    chunks = 4
    step = rows // chunks
    section = lax.axis_index("side")
    tp_index = lax.axis_index("tp")
    part = tp_index % kv_parts
    q_cols = pl.ds(
        pl.multiple_of(tp_index // kv_parts * (group_heads * HD), group_heads * HD), group_heads * HD
    )
    half_cols = pl.ds(pl.multiple_of(section * half, half), half)
    pairs = [
        (q_hbm.at[:, q_cols], q_in),
        (len_hbm, len_ref),
        *[(kv_hbm.at[pl.ds(c * step, step), 0], kv.at[pl.ds(c * step, step)]) for c in range(chunks)],
        (ids_hbm, ids_ref),
        (gates_hbm, gates_ref),
        (out_w_hbm, out_w_ref),
        (resid_hbm.at[:, half_cols], resid_ref),
        (gain_hbm, gain_ref),
    ]
    copies = [pltpu.make_async_copy(a, b, sems.at[i]) for i, (a, b) in enumerate(pairs)]
    for copy in copies:
        copy.start()
    copies[0].wait()
    for g in range(group_heads):
        q_s[pl.ds(g, rows, stride=group_heads), :] = q_in[:, g * HD : (g + 1) * HD].astype(F32)
    copies[1].wait()

    for c in range(chunks):
        copies[2 + c].wait()
        for r in range(c * step, (c + 1) * step):
            at = pl.ds(r * group_heads, group_heads)
            score_s[at, :] = lax.dot_general(
                q_s[at, :].astype(BF16),
                kv[r, :, :HD],
                (((1,), (1,)), ((), ())),
                preferred_element_type=F32,
            )
    scale = math.log2(math.e) / math.sqrt(HD)
    place = part * span + lax.broadcasted_iota(jnp.int32, (group_heads, span), 1)
    for r in range(rows):
        at = pl.ds(r * group_heads, group_heads)
        valid = place < len_ref[r]
        score = jnp.where(valid, score_s[at, :], LOW)
        top_score = jnp.max(score, axis=-1, keepdims=True)
        weight = jnp.where(valid, jnp.exp2((score - top_score) * scale), 0.0)
        max_s[at, :] = jnp.broadcast_to(top_score, (group_heads, HD))
        sum_s[at, :] = jnp.broadcast_to(jnp.sum(weight, axis=-1, keepdims=True), (group_heads, HD))
        num_s[at, :] = jnp.dot(weight.astype(BF16), kv[r, :, HD:], preferred_element_type=F32)
    lane = lax.broadcasted_iota(jnp.int32, (rows, HD), 1)
    for mask, out in enumerate([own_ref, *send_refs]):
        first = (part ^ mask) * per_member
        stats = jnp.zeros((rows, HD), F32)
        for i in range(per_member):
            pick = pl.ds(first + i, rows, stride=group_heads)
            out[:, i * HD : (i + 1) * HD] = num_s[pick, :]
            stats = jnp.where(lane == 2 * i, max_s[pick, :], stats)
            stats = jnp.where(lane == 2 * i + 1, sum_s[pick, :], stats)
        out[:, per_member * HD :] = stats
    for copy in copies[2 + chunks :]:
        copy.wait()
    place = lax.broadcasted_iota(jnp.int32, (HD, rows), 0)
    target = place % (HD // 2)
    expert = jnp.where(target < grp, ((1 - section) * grp + target) * tp + tp_index, -1)
    gate = jnp.zeros((HD, rows), F32)
    for k in range(top):
        gate = gate + jnp.where(ids_ref[k : k + 1, :] == expert, gates_ref[k : k + 1, :], 0.0)
    high = gate.astype(BF16).astype(F32)
    turn_s[...] = jnp.zeros((HD, HD), F32)
    turn_s[:, :rows] = jnp.where(place < HD // 2, high, gate - high)
    lanes_ref[...] = turn_s[...].T[:rows].astype(BF16)


def fetch_kernel(after_ref, source, target, token_ref, sems):
    parts = sems.shape[0]
    step = source.shape[1] // parts
    copies = []
    for j in range(parts):
        at = pl.ds(j * step, step)
        copies.append(pltpu.make_async_copy(source.at[:, at], target.at[:, at], sems.at[j]))
        copies[-1].start()
    token_ref[...] = after_ref[:, :HD]
    for copy in copies:
        copy.wait()


def fetched(after, weight):
    rows = after.shape[0]
    return call(
        fetch_kernel,
        [after, weight],
        [(weight.shape, BF16), ((rows, HD), BF16)],
        [pltpu.SemaphoreType.DMA((8,))],
        far=(1,),
        name="fetch",
        cost=pl.CostEstimate(flops=0, transcendentals=0, bytes_accessed=2 * weight.size),
    )


def project_kernel(sizes, token_ref, weight_ref, *rest):
    kv_parts, per_member, half, sides = sizes
    packets = rest[:kv_parts]
    away_ref, kept_ref = rest[kv_parts:]
    scale = math.log2(math.e) / math.sqrt(HD)
    heads = []
    for i in range(per_member):
        at = per_member * HD + 2 * i
        tops = [p[:, at : at + 1] for p in packets]
        whole = functools.reduce(jnp.maximum, tops)
        total, total_sum = 0.0, 0.0
        for p, top in zip(packets, tops):
            factor = jnp.exp2((top - whole) * scale)
            total = total + p[:, i * HD : (i + 1) * HD] * factor
            total_sum = total_sum + p[:, at + 1 : at + 2] * factor
        heads.append((total / total_sum).astype(BF16))
    heads = jnp.concatenate(heads, axis=1)
    section = lax.axis_index("side")
    for ref, side in ((away_ref, 1 - section), (kept_ref, section)):
        cols = pl.ds(pl.multiple_of(side * half, half), half)
        ref[...] = jnp.dot(
            heads, weight_ref[:, cols], preferred_element_type=F32
        ).astype(ref.dtype)


def add_kernel(kept_ref, came_ref, out_ref):
    out_ref[...] = (kept_ref[...] + came_ref[...].astype(F32)).astype(BF16)


def middle_kernel(half, token_ref, resid_ref, lanes_ref, *rest):
    *parts, out_ref = rest
    total = parts[0][...].astype(F32)
    for part in parts[1:]:
        total = total + part[...].astype(F32)
    out_ref[:, :half] = (resid_ref[...].astype(F32) + total).astype(BF16)
    out_ref[:, half:] = lanes_ref[...]


def gather_kernel(half, *rest):
    *packets, x_ref, gate_ref = rest
    me = lax.axis_index("grp")
    for mask, packet in enumerate(packets):
        x_ref[me ^ mask] = packet[:, :half]
        lane = lax.broadcasted_iota(jnp.int32, (packet.shape[0], HD), 1)
        picked = jnp.where(lane % (HD // 2) == me, packet[:, half:].astype(F32), 0.0)
        gate_ref[me ^ mask] = jnp.broadcast_to(
            jnp.sum(picked, axis=1, keepdims=True), (packet.shape[0], HD)
        )


def scaled_rows(x_ref, gain_ref, side, half):
    groups, rows, _ = x_ref.shape
    x = x_ref[...].astype(F32).reshape(groups * rows, half)
    gain = gain_ref[:, pl.ds(pl.multiple_of(side * half, half), half)]
    return (x * gain).astype(BF16), jnp.sum(x * x, axis=1, keepdims=True)


def first_half_kernel(tile, x_ref, gain_ref, w_ref, hidden_ref, square_ref):
    half = x_ref.shape[2]
    section = lax.axis_index("side")
    x, square = scaled_rows(x_ref, gain_ref, 1 - section, half)
    square_ref[...] = jnp.broadcast_to(square, square_ref.shape)
    rows = pl.ds(pl.multiple_of((1 - section) * half, half), half)

    def column(j, carry):
        cols = pl.ds(pl.multiple_of(j * tile, tile), tile)
        hidden_ref[:, cols] = jnp.dot(x, w_ref[0, rows, cols], preferred_element_type=F32)
        return carry

    lax.fori_loop(0, hidden_ref.shape[1] // tile, column, 0)


def second_half_kernel(
    tile, x_ref, gain_ref, w_ref, hidden_ref, square_ref, gate_ref, down_ref, act_ref, away_ref
):
    half = x_ref.shape[2]
    inner = act_ref.shape[1]
    section = lax.axis_index("side")
    x, square = scaled_rows(x_ref, gain_ref, section, half)
    square = square + square_ref[:, :1]
    inv = lax.rsqrt(square / (half * lax.axis_size("side")) + 1e-6)
    rows = pl.ds(pl.multiple_of(section * half, half), half)

    def column(j, carry):
        both = []
        for base in (0, inner):
            cols = pl.ds(pl.multiple_of(base + j * tile, tile), tile)
            part = jnp.dot(x, w_ref[0, rows, cols], preferred_element_type=F32)
            both.append((hidden_ref[:, cols] + part) * inv)
        act = both[0] / (1.0 + jnp.exp(-both[0])) * both[1]
        act_ref[:, pl.ds(pl.multiple_of(j * tile, tile), tile)] = act.astype(BF16)
        return carry

    lax.fori_loop(0, inner // tile, column, 0)
    down(tile, act_ref, gate_ref, down_ref, away_ref, 1 - section)


def down(tile, act_ref, gate_ref, down_ref, out_ref, side):
    half = out_ref.shape[1]
    gate = gate_ref[...].reshape(act_ref.shape[0], HD)[:, :1]

    def column(j, carry):
        at = pl.ds(pl.multiple_of(side * half + j * tile, tile), tile)
        part = jnp.dot(act_ref[...], down_ref[0, :, at], preferred_element_type=F32)
        out_ref[:, pl.ds(pl.multiple_of(j * tile, tile), tile)] = (part * gate).astype(
            out_ref.dtype
        )
        return carry

    lax.fori_loop(0, half // tile, column, 0)


def keep_kernel(tile, act_ref, gate_ref, down_ref, kept_ref):
    down(tile, act_ref, gate_ref, down_ref, kept_ref, lax.axis_index("side"))


def blocks_kernel(kept_ref, came_ref, out_ref):
    blocks, rows, piece = out_ref.shape
    tp = kept_ref.shape[1] // piece
    for b in range(blocks):
        at = (slice(b // tp * rows, (b // tp + 1) * rows), slice(b % tp * piece, (b % tp + 1) * piece))
        out_ref[b] = (kept_ref[at] + came_ref[at].astype(F32)).astype(BF16)


def final_kernel(blocks_ref, middle_ref, out_ref):
    blocks, rows, piece = blocks_ref.shape
    at = pl.ds(pl.multiple_of(lax.axis_index("tp") * piece, piece), piece)
    total = middle_ref[:, at].astype(F32)
    for b in range(blocks):
        total = total + blocks_ref[b].astype(F32)
    out_ref[...] = total.astype(BF16)


def body(
    queries,
    kv_cache,
    lengths,
    out_weight,
    resid,
    norm_gain,
    expert_ids,
    expert_gates,
    w_gate_up,
    w_down,
):
    tp = lax.axis_size("tp")
    grp = lax.axis_size("grp")
    sides = lax.axis_size("side")
    group_size = sides * tp
    kv_parts = group_size // KVH
    group_heads = QH // KVH
    per_member = QH // group_size
    span = kv_cache.shape[2]
    width = out_weight.shape[1]
    half = width // sides
    piece = width // group_size
    rows, top = expert_ids.shape
    inner = w_down.shape[1]
    packet = (rows, (per_member + 1) * HD)
    sizes = (tp, grp, sides, kv_parts, group_heads, per_member, rows, span, top, half)
    many = rows * group_heads
    results = call(
        functools.partial(attention_kernel, sizes),
        [
            queries,
            lengths,
            expert_ids.T,
            expert_gates.T,
            kv_cache,
            out_weight,
            resid,
            norm_gain.reshape(1, width),
        ],
        [(packet, F32)] * kv_parts
        + [
            ((rows, HD), BF16),
            (out_weight.shape, BF16),
            ((rows, half), BF16),
            ((1, width), F32),
        ],
        [
            pltpu.VMEM((rows, span, 2 * HD), BF16),
            pltpu.VMEM((rows, group_heads * HD), BF16),
            pltpu.SMEM((rows,), jnp.int32),
            pltpu.VMEM((top, rows), jnp.int32),
            pltpu.VMEM((top, rows), F32),
            pltpu.VMEM((HD, HD), F32),
            pltpu.VMEM((many, HD), F32),
            pltpu.VMEM((many, span), F32),
            pltpu.VMEM((many, HD), F32),
            pltpu.VMEM((many, HD), F32),
            pltpu.VMEM((many, HD), F32),
            pltpu.SemaphoreType.DMA((11,)),
        ],
        far=range(8),
        limit=16,
        name="attention",
    )
    own, *rest = results[:kv_parts]
    gate_lanes, out_weight, resid, gain = results[kv_parts:]
    w_down, token = fetched(gate_lanes, w_down)
    came = [swapped(rest[mask - 1], "tp", mask) for mask in range(1, kv_parts)]
    away, kept = call(
        functools.partial(project_kernel, (kv_parts, per_member, half, sides)),
        [token, out_weight, own, *came],
        [((rows, half), BF16), ((rows, half), F32)],
        name="project",
    )
    outgoing = call(add_kernel, [kept, swapped(away, "side", 1)], [((rows, half), BF16)], name="pair")[0]
    w_gate_up, token = fetched(outgoing, w_gate_up)
    parts = [outgoing] + [swapped(outgoing, "tp", mask) for mask in range(1, tp)]
    middle = call(
        functools.partial(middle_kernel, half),
        [token, resid, gate_lanes, *parts],
        [((rows, half + HD), BF16)],
        name="middle",
    )[0]
    packets = [crossed(middle, mask) for mask in range(grp)]
    far_half, gate = call(
        functools.partial(gather_kernel, half),
        packets,
        [((grp, rows, half), BF16), ((grp, rows, HD), F32)],
        name="gather",
    )
    near_half = swapped(far_half, "side", 1)
    total = grp * rows
    tile = 256
    hidden, square = call(
        functools.partial(first_half_kernel, tile),
        [far_half, gain, w_gate_up],
        [((total, 2 * inner), F32), ((total, HD), F32)],
        name="first_half",
    )
    act, sent = call(
        functools.partial(second_half_kernel, tile),
        [near_half, gain, w_gate_up, hidden, square, gate, w_down],
        [((total, inner), BF16), ((total, half), BF16)],
        name="second_half",
    )
    back = swapped(sent, "side", 1)
    mine = call(
        functools.partial(keep_kernel, tile),
        [act, gate, w_down],
        [((total, half), F32)],
        name="keep",
    )[0]
    blocks = call(
        blocks_kernel, [mine, back], [((grp * tp, rows, piece), BF16)], name="blocks"
    )[0]
    returned = lax.all_to_all(blocks, ("grp", "tp"), 0, 0, tiled=True)
    return pl.pallas_call(
        final_kernel,
        out_shape=jax.ShapeDtypeStruct((rows, piece), BF16),
        in_specs=[VMEM_SPEC] * 2,
        out_specs=VMEM_SPEC,
        name="final",
    )(near(returned), near(middle))


def solution(mesh):
    in_specs = (
        P("grp", "side"),
        P("grp", ("side", "tp"), None, None),
        P("grp"),
        P(("side", "tp"), None),
        P("grp", None),
        P(),
        P("grp", None),
        P("grp", None),
        P(("side", "grp", "tp"), None, None),
        P(("side", "grp", "tp"), None, None),
    )
    out_specs = P("grp", ("side", "tp"))
    return jax.shard_map(body, mesh=mesh, in_specs=in_specs, out_specs=out_specs, check_vma=False)
```

```python
import functools
import math

import jax
import jax.numpy as jnp
from jax import lax
from jax.experimental import pallas as pl
from jax.experimental.pallas import tpu as pltpu
from jax.sharding import PartitionSpec as P

QH = 32
KVH = 4
HD = 128
LOW = -1e30
CHUNKS = 4
LAG = 1
F32 = jnp.float32
BF16 = jnp.bfloat16
MIB = 1024 * 1024
VMEM_SPEC = pl.BlockSpec(memory_space=pltpu.VMEM)


def swapped(value, axis, mask):
    pairs = [(source, source ^ mask) for source in range(lax.axis_size(axis))]
    return lax.ppermute(value, axis, pairs)


def crossed(value, mask):
    grp, tp = lax.axis_size("grp"), lax.axis_size("tp")
    pairs = [
        ((s * grp + g) * tp + t, ((1 - s) * grp + (g ^ mask)) * tp + t)
        for s in range(2)
        for g in range(grp)
        for t in range(tp)
    ]
    return lax.ppermute(value, ("side", "grp", "tp"), pairs)


def near(value, space=pltpu.VMEM):
    return pltpu.with_memory_space_constraint(value, space)


def call(kernel, ins, outs, scratch=(), far=(), limit=8, name=None, cost=None):
    spaces = [pltpu.HBM if i in far else pltpu.VMEM for i in range(len(ins))]
    return pl.pallas_call(
        kernel,
        out_shape=[pltpu.VMEM(shape, dtype) for shape, dtype in outs],
        in_specs=[pl.BlockSpec(memory_space=s) for s in spaces],
        out_specs=[VMEM_SPEC] * len(outs),
        scratch_shapes=list(scratch),
        compiler_params=pltpu.CompilerParams(vmem_limit_bytes=limit * MIB),
        name=name,
        cost_estimate=cost,
    )(*[near(a, s) for a, s in zip(ins, spaces)])


def attention_kernel(sizes, *refs):
    tp, grp, sides, kv_parts, group_heads, per_member, rows, span, top = sizes
    q_hbm, len_hbm, ids_hbm, gates_hbm, kv_hbm = refs[:5]
    own_ref, *send_refs = refs[5 : 5 + kv_parts]
    lanes_ref = refs[5 + kv_parts]
    kv, q_in, len_ref, ids_ref, gates_ref, turn_s, q_s, score_s, num_s, max_s, sum_s, sems = refs[
        6 + kv_parts :
    ]
    step = rows // CHUNKS
    section = lax.axis_index("side")
    tp_index = lax.axis_index("tp")
    part = tp_index % kv_parts
    q_cols = pl.ds(
        pl.multiple_of(tp_index // kv_parts * (group_heads * HD), group_heads * HD), group_heads * HD
    )
    pairs = [
        (q_hbm.at[:, q_cols], q_in),
        (len_hbm, len_ref),
        (ids_hbm, ids_ref),
        (gates_hbm, gates_ref),
        *[(kv_hbm.at[pl.ds(c * step, step), 0], kv.at[pl.ds(c * step, step)]) for c in range(CHUNKS)],
    ]
    copies = [pltpu.make_async_copy(a, b, sems.at[i]) for i, (a, b) in enumerate(pairs)]
    for copy in copies:
        copy.start()
    for copy in copies[:4]:
        copy.wait()
    for g in range(group_heads):
        q_s[pl.ds(g, rows, stride=group_heads), :] = q_in[:, g * HD : (g + 1) * HD].astype(F32)
    place = lax.broadcasted_iota(jnp.int32, (HD, rows), 0)
    target = place % (HD // 2)
    expert = jnp.where(target < grp, ((1 - section) * grp + target) * tp + tp_index, -1)
    gate = jnp.zeros((HD, rows), F32)
    for k in range(top):
        gate = gate + jnp.where(ids_ref[k : k + 1, :] == expert, gates_ref[k : k + 1, :], 0.0)
    high = gate.astype(BF16).astype(F32)
    turn_s[...] = jnp.zeros((HD, HD), F32)
    turn_s[:, :rows] = jnp.where(place < HD // 2, high, gate - high)
    lanes_ref[...] = turn_s[...].T[:rows].astype(BF16)
    scale = math.log2(math.e) / math.sqrt(HD)
    place = part * span + lax.broadcasted_iota(jnp.int32, (group_heads, span), 1)
    def spot(r):
        return pl.ds(r * group_heads, group_heads)

    def values(some):
        for r in some:
            valid = place < len_ref[r]
            score = jnp.where(valid, score_s[spot(r), :], LOW)
            top_score = jnp.max(score, axis=-1, keepdims=True)
            weight = jnp.where(valid, jnp.exp2((score - top_score) * scale), 0.0)
            max_s[spot(r), :] = jnp.broadcast_to(top_score, (group_heads, HD))
            sum_s[spot(r), :] = jnp.broadcast_to(
                jnp.sum(weight, axis=-1, keepdims=True), (group_heads, HD)
            )
            num_s[spot(r), :] = jnp.dot(
                weight.astype(BF16), kv[r, :, HD:], preferred_element_type=F32
            )

    for c in range(CHUNKS):
        copies[4 + c].wait()
        for r in range(c * step, (c + 1) * step):
            score_s[spot(r), :] = lax.dot_general(
                q_s[spot(r), :].astype(BF16),
                kv[r, :, :HD],
                (((1,), (1,)), ((), ())),
                preferred_element_type=F32,
            )
        if c >= LAG:
            values(range((c - LAG) * step, (c - LAG + 1) * step))
    values(range((CHUNKS - LAG) * step, rows))
    lane = lax.broadcasted_iota(jnp.int32, (rows, HD), 1)
    for mask, out in enumerate([own_ref, *send_refs]):
        first = (part ^ mask) * per_member
        stats = jnp.zeros((rows, HD), F32)
        for i in range(per_member):
            pick = pl.ds(first + i, rows, stride=group_heads)
            out[:, i * HD : (i + 1) * HD] = num_s[pick, :].astype(out.dtype)
            for j, value in enumerate((max_s[pick, :], sum_s[pick, :])):
                for k in range(3):
                    term = value.astype(out.dtype).astype(F32)
                    stats = jnp.where(lane == 6 * i + 3 * j + k, term, stats)
                    value = value - term
        out[:, per_member * HD :] = stats.astype(out.dtype)


def fetch_kernel(parts, after_ref, *refs):
    count = (len(refs) - 2) // 2
    sources, targets, token_ref, sems = refs[:count], refs[count:-2], refs[-2], refs[-1]
    copies = []
    for source, target, number in zip(sources, targets, parts):
        axis = source.ndim - 2
        step = source.shape[axis] // number
        for j in range(number):
            at = (slice(None),) * axis + (pl.ds(j * step, step),)
            copies.append(
                pltpu.make_async_copy(source.at[at], target.at[at], sems.at[len(copies)])
            )
            copies[-1].start()
    token_ref[...] = after_ref[:, :HD]
    for copy in copies:
        copy.wait()


def fetched(after, *arrays):
    rows = after.shape[0]
    parts = [4 if a.size > MIB // 2 else 1 for a in arrays]
    return call(
        functools.partial(fetch_kernel, parts),
        [after, *arrays],
        [(a.shape, a.dtype) for a in arrays] + [((rows, HD), BF16)],
        [pltpu.SemaphoreType.DMA((sum(parts),))],
        far=range(1, len(arrays) + 1),
        name="fetch",
        cost=pl.CostEstimate(
            flops=0, transcendentals=0, bytes_accessed=sum(2 * a.size * a.dtype.itemsize for a in arrays)
        ),
    )


def project_kernel(sizes, token_ref, weight_ref, *rest):
    kv_parts, per_member, half = sizes
    packets = rest[:kv_parts]
    heads_ref, away_ref = rest[kv_parts:]
    scale = math.log2(math.e) / math.sqrt(HD)
    stats = [p[:, per_member * HD :].astype(F32) for p in packets]

    def whole(stat, at):
        return stat[:, at : at + 1] + stat[:, at + 1 : at + 2] + stat[:, at + 2 : at + 3]

    for i in range(per_member):
        tops = [whole(stat, 6 * i) for stat in stats]
        highest = functools.reduce(jnp.maximum, tops)
        total, total_sum = 0.0, 0.0
        for p, stat, top in zip(packets, stats, tops):
            factor = jnp.exp2((top - highest) * scale)
            total = total + p[:, i * HD : (i + 1) * HD].astype(F32) * factor
            total_sum = total_sum + whole(stat, 6 * i + 3) * factor
        heads_ref[:, i * HD : (i + 1) * HD] = (total / total_sum).astype(BF16)
    part_kernel(False, heads_ref, weight_ref, away_ref)


def part_kernel(mine, heads_ref, weight_ref, out_ref):
    half = out_ref.shape[1]
    section = lax.axis_index("side")
    cols = pl.ds(pl.multiple_of((section if mine else 1 - section) * half, half), half)
    out_ref[...] = jnp.dot(
        heads_ref[...], weight_ref[:, cols], preferred_element_type=F32
    ).astype(out_ref.dtype)


def add_kernel(kept_ref, came_ref, out_ref):
    out_ref[...] = (kept_ref[...] + came_ref[...].astype(F32)).astype(BF16)


def middle_kernel(half, token_ref, resid_ref, lanes_ref, *rest):
    *parts, out_ref = rest
    cols = pl.ds(pl.multiple_of(lax.axis_index("side") * half, half), half)
    total = parts[0][...].astype(F32)
    for part in parts[1:]:
        total = total + part[...].astype(F32)
    out_ref[:, :half] = (resid_ref[:, cols].astype(F32) + total).astype(BF16)
    out_ref[:, half:] = lanes_ref[...]


def gather_kernel(half, token_ref, *rest):
    *packets, x_ref, gate_ref = rest
    me = lax.axis_index("grp")
    for mask, packet in enumerate(packets):
        x_ref[me ^ mask] = packet[:, :half]
        lane = lax.broadcasted_iota(jnp.int32, (packet.shape[0], HD), 1)
        picked = jnp.where(lane % (HD // 2) == me, packet[:, half:].astype(F32), 0.0)
        gate_ref[me ^ mask] = jnp.broadcast_to(
            jnp.sum(picked, axis=1, keepdims=True), (packet.shape[0], HD)
        )


def scaled_rows(x_ref, gain_ref, side, half):
    groups, rows, _ = x_ref.shape
    x = x_ref[...].astype(F32).reshape(groups * rows, half)
    gain = gain_ref[:, pl.ds(pl.multiple_of(side * half, half), half)]
    return (x * gain).astype(BF16), jnp.sum(x * x, axis=1, keepdims=True)


def first_half_kernel(tile, x_ref, gain_ref, w_ref, hidden_ref, square_ref):
    half = x_ref.shape[2]
    section = lax.axis_index("side")
    x, square = scaled_rows(x_ref, gain_ref, 1 - section, half)
    square_ref[...] = jnp.broadcast_to(square, square_ref.shape)
    rows = pl.ds(pl.multiple_of((1 - section) * half, half), half)

    def column(j, carry):
        cols = pl.ds(j * tile, tile)
        hidden_ref[:, cols] = jnp.dot(x, w_ref[0, rows, cols], preferred_element_type=F32)
        return carry

    for j in range(hidden_ref.shape[1] // tile):
        column(j, 0)


def second_half_kernel(
    tile, x_ref, gain_ref, w_ref, hidden_ref, square_ref, gate_ref, down_ref, act_ref, away_ref
):
    half = x_ref.shape[2]
    inner = act_ref.shape[1]
    section = lax.axis_index("side")
    x, square = scaled_rows(x_ref, gain_ref, section, half)
    square = square + square_ref[:, :1]
    inv = lax.rsqrt(square / (half * lax.axis_size("side")) + 1e-6)
    rows = pl.ds(pl.multiple_of(section * half, half), half)

    def column(j, carry):
        both = []
        for base in (0, inner):
            cols = pl.ds(base + j * tile, tile)
            part = jnp.dot(x, w_ref[0, rows, cols], preferred_element_type=F32)
            both.append((hidden_ref[:, cols] + part) * inv)
        act = both[0] / (1.0 + jnp.exp(-both[0])) * both[1]
        act_ref[:, pl.ds(j * tile, tile)] = act.astype(BF16)
        return carry

    for j in range(inner // tile):
        column(j, 0)
    down(tile, act_ref, gate_ref, down_ref, away_ref, 1 - section)


def down(tile, act_ref, gate_ref, down_ref, out_ref, side):
    half = out_ref.shape[1]
    gate = gate_ref[...].reshape(act_ref.shape[0], HD)[:, :1]

    def column(j, carry):
        at = pl.ds(pl.multiple_of(side * half + j * tile, HD), tile)
        part = jnp.dot(act_ref[...], down_ref[0, :, at], preferred_element_type=F32)
        out_ref[:, pl.ds(j * tile, tile)] = (part * gate).astype(
            out_ref.dtype
        )
        return carry

    for j in range(half // tile):
        column(j, 0)


def keep_kernel(tile, act_ref, gate_ref, down_ref, kept_ref):
    down(tile, act_ref, gate_ref, down_ref, kept_ref, lax.axis_index("side"))


def blocks_kernel(kept_ref, came_ref, out_ref):
    blocks, rows, piece = out_ref.shape
    tp = kept_ref.shape[1] // piece
    for b in range(blocks):
        at = (slice(b // tp * rows, (b // tp + 1) * rows), slice(b % tp * piece, (b % tp + 1) * piece))
        out_ref[b] = (kept_ref[at] + came_ref[at].astype(F32)).astype(BF16)


def final_kernel(blocks_ref, middle_ref, out_ref):
    blocks, rows, piece = blocks_ref.shape
    at = pl.ds(pl.multiple_of(lax.axis_index("tp") * piece, piece), piece)
    total = middle_ref[:, at].astype(F32)
    for b in range(blocks):
        total = total + blocks_ref[b].astype(F32)
    out_ref[...] = total.astype(BF16)


def body(
    queries,
    kv_cache,
    lengths,
    out_weight,
    resid,
    norm_gain,
    expert_ids,
    expert_gates,
    w_gate_up,
    w_down,
):
    tp = lax.axis_size("tp")
    grp = lax.axis_size("grp")
    sides = lax.axis_size("side")
    group_size = sides * tp
    kv_parts = group_size // KVH
    group_heads = QH // KVH
    per_member = QH // group_size
    span = kv_cache.shape[2]
    width = out_weight.shape[1]
    half = width // sides
    piece = width // group_size
    rows, top = expert_ids.shape
    inner = w_down.shape[1]
    packet = (rows, (per_member + 1) * HD)
    sizes = (tp, grp, sides, kv_parts, group_heads, per_member, rows, span, top)
    many = rows * group_heads
    results = call(
        functools.partial(attention_kernel, sizes),
        [
            queries,
            lengths,
            expert_ids.T,
            expert_gates.T,
            kv_cache,
        ],
        [(packet, F32)] + [(packet, BF16)] * (kv_parts - 1)
        + [((rows, HD), BF16)],
        [
            pltpu.VMEM((rows, span, 2 * HD), BF16),
            pltpu.VMEM((rows, group_heads * HD), BF16),
            pltpu.SMEM((rows,), jnp.int32),
            pltpu.VMEM((top, rows), jnp.int32),
            pltpu.VMEM((top, rows), F32),
            pltpu.VMEM((HD, HD), F32),
            pltpu.VMEM((many, HD), F32),
            pltpu.VMEM((many, span), F32),
            pltpu.VMEM((many, HD), F32),
            pltpu.VMEM((many, HD), F32),
            pltpu.VMEM((many, HD), F32),
            pltpu.SemaphoreType.DMA((4 + CHUNKS,)),
        ],
        far=range(5),
        limit=16,
        name="attention",
    )
    own, *rest = results[:kv_parts]
    gate_lanes = results[kv_parts]
    out_weight, resid, gain, token = fetched(
        gate_lanes, out_weight, resid, norm_gain.reshape(1, width)
    )
    came = [swapped(rest[mask - 1], "tp", mask) for mask in range(1, kv_parts)]
    heads, away = call(
        functools.partial(project_kernel, (kv_parts, per_member, half)),
        [token, out_weight, own, *came],
        [((rows, per_member * HD), BF16), ((rows, half), BF16)],
        name="project",
    )
    away = swapped(away, "side", 1)
    kept = call(
        functools.partial(part_kernel, True), [heads, out_weight], [((rows, half), F32)], name="kept"
    )[0]
    outgoing = call(add_kernel, [kept, away], [((rows, half), BF16)], name="pair")[0]
    w_gate_up, token = fetched(outgoing, w_gate_up)
    parts = [outgoing] + [swapped(outgoing, "tp", mask) for mask in range(1, tp)]
    middle = call(
        functools.partial(middle_kernel, half),
        [token, resid, gate_lanes, *parts],
        [((rows, half + HD), BF16)],
        name="middle",
    )[0]
    w_down, token = fetched(middle, w_down)
    packets = [crossed(middle, mask) for mask in [*range(1, grp), 0]]
    packets = [packets[-1], *packets[:-1]]
    far_half, gate = call(
        functools.partial(gather_kernel, half),
        [token, *packets],
        [((grp, rows, half), BF16), ((grp, rows, HD), F32)],
        name="gather",
    )
    near_half = swapped(far_half, "side", 1)
    total = grp * rows
    tile = 256
    hidden, square = call(
        functools.partial(first_half_kernel, tile),
        [far_half, gain, w_gate_up],
        [((total, 2 * inner), F32), ((total, HD), F32)],
        name="first_half",
    )
    act, sent = call(
        functools.partial(second_half_kernel, tile),
        [near_half, gain, w_gate_up, hidden, square, gate, w_down],
        [((total, inner), BF16), ((total, half), BF16)],
        name="second_half",
    )
    back = swapped(sent, "side", 1)
    mine = call(
        functools.partial(keep_kernel, tile),
        [act, gate, w_down],
        [((total, half), F32)],
        name="keep",
    )[0]
    blocks = call(
        blocks_kernel, [mine, back], [((grp * tp, rows, piece), BF16)], name="blocks"
    )[0]
    returned = lax.all_to_all(blocks, ("grp", "tp"), 0, 0, tiled=True)
    return pl.pallas_call(
        final_kernel,
        out_shape=jax.ShapeDtypeStruct((rows, piece), BF16),
        in_specs=[VMEM_SPEC] * 2,
        out_specs=VMEM_SPEC,
        name="final",
    )(near(returned), near(middle))


def solution(mesh):
    in_specs = (
        P("grp", "side"),
        P("grp", ("side", "tp"), None, None),
        P("grp"),
        P(("side", "tp"), None),
        P("grp", None),
        P(),
        P("grp", None),
        P("grp", None),
        P(("side", "grp", "tp"), None, None),
        P(("side", "grp", "tp"), None, None),
    )
    out_specs = P("grp", ("side", "tp"))
    return jax.shard_map(body, mesh=mesh, in_specs=in_specs, out_specs=out_specs, check_vma=False)
```

```python
import functools
import math

import jax
import jax.numpy as jnp
from jax import lax
from jax.experimental import pallas as pl
from jax.experimental.pallas import tpu as pltpu
from jax.sharding import PartitionSpec as P

QH = 32
KVH = 4
HD = 128
LOW = -1e30
CHUNKS = 4
LAG = 1
F32 = jnp.float32
BF16 = jnp.bfloat16
MIB = 1024 * 1024
VMEM_SPEC = pl.BlockSpec(memory_space=pltpu.VMEM)


def swapped(value, axis, mask):
    pairs = [(source, source ^ mask) for source in range(lax.axis_size(axis))]
    return lax.ppermute(value, axis, pairs)


def crossed(value, mask, along=0):
    grp, tp = lax.axis_size("grp"), lax.axis_size("tp")
    pairs = [
        ((s * grp + g) * tp + t, ((1 - s) * grp + (g ^ mask)) * tp + (t ^ along))
        for s in range(2)
        for g in range(grp)
        for t in range(tp)
    ]
    return lax.ppermute(value, ("side", "grp", "tp"), pairs)


def near(value, space=pltpu.VMEM):
    return pltpu.with_memory_space_constraint(value, space)


def call(kernel, ins, outs, scratch=(), far=(), limit=8, name=None, cost=None):
    spaces = [pltpu.HBM if i in far else pltpu.VMEM for i in range(len(ins))]
    return pl.pallas_call(
        kernel,
        out_shape=[pltpu.VMEM(shape, dtype) for shape, dtype in outs],
        in_specs=[pl.BlockSpec(memory_space=s) for s in spaces],
        out_specs=[VMEM_SPEC] * len(outs),
        scratch_shapes=list(scratch),
        compiler_params=pltpu.CompilerParams(vmem_limit_bytes=limit * MIB),
        name=name,
        cost_estimate=cost,
    )(*[near(a, s) for a, s in zip(ins, spaces)])


def attention_kernel(sizes, *refs):
    tp, grp, sides, kv_parts, group_heads, per_member, rows, span, top = sizes
    q_hbm, len_hbm, ids_hbm, gates_hbm, kv_hbm = refs[:5]
    own_ref, *send_refs = refs[5 : 5 + kv_parts]
    lanes_ref = refs[5 + kv_parts]
    kv, q_in, len_ref, ids_ref, gates_ref, turn_s, q_s, score_s, num_s, max_s, sum_s, sems = refs[
        6 + kv_parts :
    ]
    step = rows // CHUNKS
    section = lax.axis_index("side")
    tp_index = lax.axis_index("tp")
    part = tp_index % kv_parts
    q_cols = pl.ds(
        pl.multiple_of(tp_index // kv_parts * (group_heads * HD), group_heads * HD), group_heads * HD
    )
    pairs = [
        (q_hbm.at[:, q_cols], q_in),
        (len_hbm, len_ref),
        (ids_hbm, ids_ref),
        (gates_hbm, gates_ref),
        *[(kv_hbm.at[pl.ds(c * step, step), 0], kv.at[pl.ds(c * step, step)]) for c in range(CHUNKS)],
    ]
    copies = [pltpu.make_async_copy(a, b, sems.at[i]) for i, (a, b) in enumerate(pairs)]
    for copy in copies:
        copy.start()
    for copy in copies[:4]:
        copy.wait()
    for g in range(group_heads):
        q_s[pl.ds(g, rows, stride=group_heads), :] = q_in[:, g * HD : (g + 1) * HD].astype(F32)
    place = lax.broadcasted_iota(jnp.int32, (HD, rows), 0)
    target = place % (HD // 2)
    expert = jnp.where(target < grp, ((1 - section) * grp + target) * tp + tp_index, -1)
    gate = jnp.zeros((HD, rows), F32)
    for k in range(top):
        gate = gate + jnp.where(ids_ref[k : k + 1, :] == expert, gates_ref[k : k + 1, :], 0.0)
    high = gate.astype(BF16).astype(F32)
    turn_s[...] = jnp.zeros((HD, HD), F32)
    turn_s[:, :rows] = jnp.where(place < HD // 2, high, gate - high)
    lanes_ref[...] = turn_s[...].T[:rows].astype(BF16)
    scale = math.log2(math.e) / math.sqrt(HD)
    place = part * span + lax.broadcasted_iota(jnp.int32, (group_heads, span), 1)
    def spot(r):
        return pl.ds(r * group_heads, group_heads)

    def values(some):
        for r in some:
            valid = place < len_ref[r]
            score = jnp.where(valid, score_s[spot(r), :], LOW)
            top_score = jnp.max(score, axis=-1, keepdims=True)
            weight = jnp.where(valid, jnp.exp2((score - top_score) * scale), 0.0)
            max_s[spot(r), :] = jnp.broadcast_to(top_score, (group_heads, HD))
            sum_s[spot(r), :] = jnp.broadcast_to(
                jnp.sum(weight, axis=-1, keepdims=True), (group_heads, HD)
            )
            num_s[spot(r), :] = jnp.dot(
                weight.astype(BF16), kv[r, :, HD:], preferred_element_type=F32
            )

    for c in range(CHUNKS):
        copies[4 + c].wait()
        for r in range(c * step, (c + 1) * step):
            score_s[spot(r), :] = lax.dot_general(
                q_s[spot(r), :].astype(BF16),
                kv[r, :, :HD],
                (((1,), (1,)), ((), ())),
                preferred_element_type=F32,
            )
        if c >= LAG:
            values(range((c - LAG) * step, (c - LAG + 1) * step))
    values(range((CHUNKS - LAG) * step, rows))
    lane = lax.broadcasted_iota(jnp.int32, (rows, HD), 1)
    for mask, out in enumerate([own_ref, *send_refs]):
        first = (part ^ mask) * per_member
        stats = jnp.zeros((rows, HD), F32)
        for i in range(per_member):
            pick = pl.ds(first + i, rows, stride=group_heads)
            out[:, i * HD : (i + 1) * HD] = num_s[pick, :].astype(out.dtype)
            for j, value in enumerate((max_s[pick, :], sum_s[pick, :])):
                for k in range(3):
                    term = value.astype(out.dtype).astype(F32)
                    stats = jnp.where(lane == 6 * i + 3 * j + k, term, stats)
                    value = value - term
        out[:, per_member * HD :] = stats.astype(out.dtype)


def fetch_kernel(parts, after_ref, *refs):
    count = (len(refs) - 2) // 2
    sources, targets, token_ref, sems = refs[:count], refs[count:-2], refs[-2], refs[-1]
    copies = []
    for source, target, number in zip(sources, targets, parts):
        axis = source.ndim - 2
        step = source.shape[axis] // number
        for j in range(number):
            at = (slice(None),) * axis + (pl.ds(j * step, step),)
            copies.append(
                pltpu.make_async_copy(source.at[at], target.at[at], sems.at[len(copies)])
            )
            copies[-1].start()
    token_ref[...] = after_ref[:, :HD]
    for copy in copies:
        copy.wait()


def fetched(after, *arrays):
    rows = after.shape[0]
    parts = [4 if a.size > MIB // 2 else 1 for a in arrays]
    return call(
        functools.partial(fetch_kernel, parts),
        [after, *arrays],
        [(a.shape, a.dtype) for a in arrays] + [((rows, HD), BF16)],
        [pltpu.SemaphoreType.DMA((sum(parts),))],
        far=range(1, len(arrays) + 1),
        name="fetch",
        cost=pl.CostEstimate(
            flops=0, transcendentals=0, bytes_accessed=sum(2 * a.size * a.dtype.itemsize for a in arrays)
        ),
    )


def project_kernel(sizes, token_ref, weight_ref, *rest):
    kv_parts, per_member, half = sizes
    packets = rest[:kv_parts]
    heads_ref, away_ref = rest[kv_parts:]
    scale = math.log2(math.e) / math.sqrt(HD)
    stats = [p[:, per_member * HD :].astype(F32) for p in packets]

    def whole(stat, at):
        return stat[:, at : at + 1] + stat[:, at + 1 : at + 2] + stat[:, at + 2 : at + 3]

    for i in range(per_member):
        tops = [whole(stat, 6 * i) for stat in stats]
        highest = functools.reduce(jnp.maximum, tops)
        total, total_sum = 0.0, 0.0
        for p, stat, top in zip(packets, stats, tops):
            factor = jnp.exp2((top - highest) * scale)
            total = total + p[:, i * HD : (i + 1) * HD].astype(F32) * factor
            total_sum = total_sum + whole(stat, 6 * i + 3) * factor
        heads_ref[:, i * HD : (i + 1) * HD] = (total / total_sum).astype(BF16)
    part_kernel(False, heads_ref, weight_ref, away_ref)


def part_kernel(mine, heads_ref, weight_ref, out_ref):
    half = out_ref.shape[1]
    section = lax.axis_index("side")
    cols = pl.ds(pl.multiple_of((section if mine else 1 - section) * half, half), half)
    out_ref[...] = jnp.dot(
        heads_ref[...], weight_ref[:, cols], preferred_element_type=F32
    ).astype(out_ref.dtype)


def add_kernel(kept_ref, came_ref, out_ref):
    out_ref[...] = (kept_ref[...] + came_ref[...].astype(F32)).astype(BF16)


def middle_kernel(half, token_ref, resid_ref, lanes_ref, *rest):
    *parts, out_ref = rest
    cols = pl.ds(pl.multiple_of(lax.axis_index("side") * half, half), half)
    total = parts[0][...].astype(F32)
    for part in parts[1:]:
        total = total + part[...].astype(F32)
    out_ref[:, :half] = (resid_ref[:, cols].astype(F32) + total).astype(BF16)
    out_ref[:, half:] = lanes_ref[...]


def scaled_rows(packets, gain_ref, side, half):
    x = jnp.concatenate([p[:, :half].astype(F32) for p in packets], axis=0)
    gain = gain_ref[:, pl.ds(pl.multiple_of(side * half, half), half)]
    return (x * gain).astype(BF16), jnp.sum(x * x, axis=1, keepdims=True)


def first_half_kernel(tile, half, gain_ref, w_ref, *rest):
    *packets, hidden_ref, square_ref, gate_ref = rest
    section = lax.axis_index("side")
    me = lax.axis_index("grp")
    x, square = scaled_rows(packets, gain_ref, 1 - section, half)
    square_ref[...] = jnp.broadcast_to(square, square_ref.shape)
    lanes = jnp.concatenate([p[:, half:].astype(F32) for p in packets], axis=0)
    lane = lax.broadcasted_iota(jnp.int32, lanes.shape, 1)
    gate = jnp.sum(jnp.where(lane % (HD // 2) == me, lanes, 0.0), axis=1, keepdims=True)
    gate_ref[...] = jnp.broadcast_to(gate, gate_ref.shape)
    rows = pl.ds(pl.multiple_of((1 - section) * half, half), half)

    def column(j, carry):
        cols = pl.ds(j * tile, tile)
        hidden_ref[:, cols] = jnp.dot(x, w_ref[0, rows, cols], preferred_element_type=F32)
        return carry

    for j in range(hidden_ref.shape[1] // tile):
        column(j, 0)


def second_half_kernel(
    tile, half, gain_ref, w_ref, hidden_ref, square_ref, gate_ref, down_ref, *rest
):
    *packets, act_ref, away_ref = rest
    inner = act_ref.shape[1]
    section = lax.axis_index("side")
    x, square = scaled_rows(packets, gain_ref, section, half)
    square = square + square_ref[:, :1]
    inv = lax.rsqrt(square / (half * lax.axis_size("side")) + 1e-6)
    rows = pl.ds(pl.multiple_of(section * half, half), half)

    def column(j, carry):
        both = []
        for base in (0, inner):
            cols = pl.ds(base + j * tile, tile)
            part = jnp.dot(x, w_ref[0, rows, cols], preferred_element_type=F32)
            both.append((hidden_ref[:, cols] + part) * inv)
        act = both[0] / (1.0 + jnp.exp(-both[0])) * both[1]
        act_ref[:, pl.ds(j * tile, tile)] = act.astype(BF16)
        return carry

    for j in range(inner // tile):
        column(j, 0)
    down(tile, act_ref, gate_ref, down_ref, away_ref, 1 - section)


def down(tile, act_ref, gate_ref, down_ref, out_ref, side):
    half = out_ref.shape[1]
    gate = gate_ref[:, :1]

    def column(j, carry):
        at = pl.ds(pl.multiple_of(side * half + j * tile, HD), tile)
        part = jnp.dot(act_ref[...], down_ref[0, :, at], preferred_element_type=F32)
        out_ref[:, pl.ds(j * tile, tile)] = (part * gate).astype(
            out_ref.dtype
        )
        return carry

    for j in range(half // tile):
        column(j, 0)


def keep_kernel(tile, act_ref, gate_ref, down_ref, kept_ref):
    down(tile, act_ref, gate_ref, down_ref, kept_ref, lax.axis_index("side"))


def fold_kernel(rows, kept_ref, came_ref, *sends):
    for b, ref in enumerate(sends):
        at = slice(b * rows, (b + 1) * rows)
        ref[...] = (kept_ref[at, :] + came_ref[at, :].astype(F32)).astype(BF16)


def split_kernel(count, *refs):
    parts, sends = refs[:count], refs[count:]
    piece = sends[0].shape[1]
    me = lax.axis_index("tp")
    for mask, ref in enumerate(sends):
        at = pl.ds(pl.multiple_of((me ^ mask) * piece, piece), piece)
        total = parts[0][:, at].astype(F32)
        for part in parts[1:]:
            total = total + part[:, at].astype(F32)
        ref[...] = total.astype(BF16)


def final_kernel(middle_ref, *rest):
    *parts, out_ref = rest
    piece = out_ref.shape[1]
    at = pl.ds(pl.multiple_of(lax.axis_index("tp") * piece, piece), piece)
    total = middle_ref[:, at].astype(F32)
    for part in parts:
        total = total + part[...].astype(F32)
    out_ref[...] = total.astype(BF16)


def body(
    queries,
    kv_cache,
    lengths,
    out_weight,
    resid,
    norm_gain,
    expert_ids,
    expert_gates,
    w_gate_up,
    w_down,
):
    tp = lax.axis_size("tp")
    grp = lax.axis_size("grp")
    sides = lax.axis_size("side")
    group_size = sides * tp
    kv_parts = group_size // KVH
    group_heads = QH // KVH
    per_member = QH // group_size
    span = kv_cache.shape[2]
    width = out_weight.shape[1]
    half = width // sides
    piece = width // group_size
    rows, top = expert_ids.shape
    inner = w_down.shape[1]
    packet = (rows, (per_member + 1) * HD)
    sizes = (tp, grp, sides, kv_parts, group_heads, per_member, rows, span, top)
    many = rows * group_heads
    results = call(
        functools.partial(attention_kernel, sizes),
        [
            queries,
            lengths,
            expert_ids.T,
            expert_gates.T,
            kv_cache,
        ],
        [(packet, F32)] + [(packet, BF16)] * (kv_parts - 1)
        + [((rows, HD), BF16)],
        [
            pltpu.VMEM((rows, span, 2 * HD), BF16),
            pltpu.VMEM((rows, group_heads * HD), BF16),
            pltpu.SMEM((rows,), jnp.int32),
            pltpu.VMEM((top, rows), jnp.int32),
            pltpu.VMEM((top, rows), F32),
            pltpu.VMEM((HD, HD), F32),
            pltpu.VMEM((many, HD), F32),
            pltpu.VMEM((many, span), F32),
            pltpu.VMEM((many, HD), F32),
            pltpu.VMEM((many, HD), F32),
            pltpu.VMEM((many, HD), F32),
            pltpu.SemaphoreType.DMA((4 + CHUNKS,)),
        ],
        far=range(5),
        limit=16,
        name="attention",
    )
    own, *rest = results[:kv_parts]
    gate_lanes = results[kv_parts]
    out_weight, resid, gain, token = fetched(
        gate_lanes, out_weight, resid, norm_gain.reshape(1, width)
    )
    came = [swapped(rest[mask - 1], "tp", mask) for mask in range(1, kv_parts)]
    heads, away = call(
        functools.partial(project_kernel, (kv_parts, per_member, half)),
        [token, out_weight, own, *came],
        [((rows, per_member * HD), BF16), ((rows, half), BF16)],
        name="project",
    )
    away = swapped(away, "side", 1)
    kept = call(
        functools.partial(part_kernel, True), [heads, out_weight], [((rows, half), F32)], name="kept"
    )[0]
    outgoing = call(add_kernel, [kept, away], [((rows, half), BF16)], name="pair")[0]
    w_gate_up, token = fetched(outgoing, w_gate_up)
    parts = [outgoing] + [swapped(outgoing, "tp", mask) for mask in range(1, tp)]
    middle = call(
        functools.partial(middle_kernel, half),
        [token, resid, gate_lanes, *parts],
        [((rows, half + HD), BF16)],
        name="middle",
    )[0]
    packets = [crossed(middle, mask) for mask in [*range(1, grp), 0]]
    packets = [packets[-1], *packets[:-1]]
    near_packets = [middle] + [swapped(p, "side", 1) for p in packets[1:]]
    total = grp * rows
    tile = 256
    hidden, square, gate = call(
        functools.partial(first_half_kernel, tile, half),
        [gain, w_gate_up, *packets],
        [((total, 2 * inner), F32), ((total, HD), F32), ((total, HD), F32)],
        name="first_half",
    )
    act, sent = call(
        functools.partial(second_half_kernel, tile, half),
        [gain, w_gate_up, hidden, square, gate, w_down, *near_packets],
        [((total, inner), BF16), ((total, half), BF16)],
        name="second_half",
    )
    back = swapped(sent, "side", 1)
    mine = call(
        functools.partial(keep_kernel, tile),
        [act, gate, w_down],
        [((total, half), F32)],
        name="keep",
    )[0]
    sends = call(
        functools.partial(fold_kernel, rows),
        [mine, back],
        [((rows, half), BF16)] * grp,
        name="fold",
    )
    came = [crossed(sends[mask], mask) for mask in reversed(range(grp))]
    sends = call(
        functools.partial(split_kernel, grp),
        came,
        [((rows, piece), BF16)] * tp,
        name="split",
    )
    came = [crossed(sends[mask], 0, mask) for mask in reversed(range(tp))]
    ins = [middle, *came]
    return pl.pallas_call(
        final_kernel,
        out_shape=jax.ShapeDtypeStruct((rows, piece), BF16),
        in_specs=[VMEM_SPEC] * len(ins),
        out_specs=VMEM_SPEC,
        name="final",
    )(*map(near, ins))


def solution(mesh):
    in_specs = (
        P("grp", "side"),
        P("grp", ("side", "tp"), None, None),
        P("grp"),
        P(("side", "tp"), None),
        P("grp", None),
        P(),
        P("grp", None),
        P("grp", None),
        P(("side", "grp", "tp"), None, None),
        P(("side", "grp", "tp"), None, None),
    )
    out_specs = P("grp", ("side", "tp"))
    return jax.shard_map(body, mesh=mesh, in_specs=in_specs, out_specs=out_specs, check_vma=False)
```

```python
import functools
import math

import jax
import jax.numpy as jnp
from jax import lax
from jax.experimental import pallas as pl
from jax.experimental.pallas import tpu as pltpu
from jax.sharding import PartitionSpec as P

QH = 32
KVH = 4
HD = 128
LOW = -1e30
SUMS = 16
TERM = 32
CUTS = (0, 6, 12, 18, 24)
CUT_OF = 24
LAG = 1
F32 = jnp.float32
BF16 = jnp.bfloat16
MIB = 1024 * 1024
VMEM_SPEC = pl.BlockSpec(memory_space=pltpu.VMEM)


def swapped(value, axis, mask):
    pairs = [(source, source ^ mask) for source in range(lax.axis_size(axis))]
    return lax.ppermute(value, axis, pairs)


def crossed(value, mask, along=0):
    grp, tp = lax.axis_size("grp"), lax.axis_size("tp")
    pairs = [
        ((s * grp + g) * tp + t, ((1 - s) * grp + (g ^ mask)) * tp + (t ^ along))
        for s in range(2)
        for g in range(grp)
        for t in range(tp)
    ]
    return lax.ppermute(value, ("side", "grp", "tp"), pairs)


def near(value, space=pltpu.VMEM):
    return pltpu.with_memory_space_constraint(value, space)


def call(kernel, ins, outs, scratch=(), far=(), limit=8, name=None, cost=None):
    spaces = [pltpu.HBM if i in far else pltpu.VMEM for i in range(len(ins))]
    return pl.pallas_call(
        kernel,
        out_shape=[pltpu.VMEM(shape, dtype) for shape, dtype in outs],
        in_specs=[pl.BlockSpec(memory_space=s) for s in spaces],
        out_specs=[VMEM_SPEC] * len(outs),
        scratch_shapes=list(scratch),
        compiler_params=pltpu.CompilerParams(vmem_limit_bytes=limit * MIB),
        name=name,
        cost_estimate=cost,
    )(*[near(a, s) for a, s in zip(ins, spaces)])


def attention_kernel(sizes, *refs):
    tp, grp, sides, kv_parts, group_heads, per_member, rows, span, top = sizes
    q_hbm, len_hbm, ids_hbm, gates_hbm, kv_hbm = refs[:5]
    own_ref, *send_refs = refs[5 : 5 + kv_parts]
    lanes_ref = refs[5 + kv_parts]
    kv, q_in, len_ref, ids_ref, gates_ref, turn_s, q_s, score_s, num_s, max_s, sum_s, sems = refs[
        6 + kv_parts :
    ]
    cuts = [rows * c // CUT_OF for c in CUTS]
    chunks = list(zip(cuts, cuts[1:]))
    section = lax.axis_index("side")
    tp_index = lax.axis_index("tp")
    part = tp_index % kv_parts
    q_cols = pl.ds(
        pl.multiple_of(tp_index // kv_parts * (group_heads * HD), group_heads * HD), group_heads * HD
    )
    pairs = [
        (q_hbm.at[:, q_cols], q_in),
        (len_hbm, len_ref),
        (ids_hbm, ids_ref),
        (gates_hbm, gates_ref),
        *[(kv_hbm.at[pl.ds(a, b - a), 0], kv.at[pl.ds(a, b - a)]) for a, b in chunks],
    ]
    copies = [pltpu.make_async_copy(a, b, sems.at[i]) for i, (a, b) in enumerate(pairs)]
    for copy in copies:
        copy.start()
    for copy in copies[:4]:
        copy.wait()
    for g in range(group_heads):
        q_s[pl.ds(g, rows, stride=group_heads), :] = q_in[:, g * HD : (g + 1) * HD].astype(F32)
    place = lax.broadcasted_iota(jnp.int32, (HD, rows), 0)
    target = place % (HD // 2)
    expert = jnp.where(target < grp, ((1 - section) * grp + target) * tp + tp_index, -1)
    gate = jnp.zeros((HD, rows), F32)
    for k in range(top):
        gate = gate + jnp.where(ids_ref[k : k + 1, :] == expert, gates_ref[k : k + 1, :], 0.0)
    high = gate.astype(BF16).astype(F32)
    turn_s[...] = jnp.zeros((HD, HD), F32)
    turn_s[:, :rows] = jnp.where(place < HD // 2, high, gate - high)
    lanes_ref[...] = turn_s[...].T[:rows].astype(BF16)
    scale = math.log2(math.e) / math.sqrt(HD)
    place = part * span + lax.broadcasted_iota(jnp.int32, (group_heads, span), 1)
    def spot(r):
        return pl.ds(r * group_heads, group_heads)

    def values(some):
        for r in some:
            valid = place < len_ref[r]
            score = jnp.where(valid, score_s[spot(r), :], LOW)
            top_score = jnp.max(score, axis=-1, keepdims=True)
            weight = jnp.where(valid, jnp.exp2((score - top_score) * scale), 0.0)
            max_s[spot(r), :] = jnp.broadcast_to(top_score, (group_heads, HD))
            sum_s[spot(r), :] = jnp.broadcast_to(
                jnp.sum(weight, axis=-1, keepdims=True), (group_heads, HD)
            )
            num_s[spot(r), :] = jnp.dot(
                weight.astype(BF16), kv[r, :, HD:], preferred_element_type=F32
            )

    for c, span_of in enumerate(chunks):
        copies[4 + c].wait()
        for r in range(*span_of):
            score_s[spot(r), :] = lax.dot_general(
                q_s[spot(r), :].astype(BF16),
                kv[r, :, :HD],
                (((1,), (1,)), ((), ())),
                preferred_element_type=F32,
            )
        if c >= LAG:
            values(range(*chunks[c - LAG]))
    values(range(cuts[-1 - LAG], rows))
    lane = lax.broadcasted_iota(jnp.int32, (rows, HD), 1)
    for mask, out in enumerate([own_ref, *send_refs]):
        first = (part ^ mask) * per_member
        stats = jnp.zeros((rows, HD), F32)
        for i in range(per_member):
            pick = pl.ds(first + i, rows, stride=group_heads)
            out[:, i * HD : (i + 1) * HD] = num_s[pick, :].astype(out.dtype)
            stats = jnp.where(lane == i, max_s[pick, :], stats)
            stats = jnp.where(lane == SUMS + i, sum_s[pick, :], stats)
        sent = jnp.zeros((rows, HD), F32)
        for k in range(3):
            term = stats.astype(out.dtype).astype(F32)
            sent = sent + (pltpu.roll(term, k * TERM, 1) if k else term)
            stats = stats - term
        out[:, per_member * HD :] = sent.astype(out.dtype)


def fetch_kernel(parts, after_ref, *refs):
    count = (len(refs) - 2) // 2
    sources, targets, token_ref, sems = refs[:count], refs[count:-2], refs[-2], refs[-1]
    copies = []
    for source, target, number in zip(sources, targets, parts):
        axis = source.ndim - 2
        step = source.shape[axis] // number
        for j in range(number):
            at = (slice(None),) * axis + (pl.ds(j * step, step),)
            copies.append(
                pltpu.make_async_copy(source.at[at], target.at[at], sems.at[len(copies)])
            )
            copies[-1].start()
    token_ref[...] = after_ref[:, :HD]
    for copy in copies:
        copy.wait()


def fetched(after, *arrays):
    rows = after.shape[0]
    parts = [4 if a.size > MIB // 2 else 1 for a in arrays]
    return call(
        functools.partial(fetch_kernel, parts),
        [after, *arrays],
        [(a.shape, a.dtype) for a in arrays] + [((rows, HD), BF16)],
        [pltpu.SemaphoreType.DMA((sum(parts),))],
        far=range(1, len(arrays) + 1),
        name="fetch",
        cost=pl.CostEstimate(
            flops=0, transcendentals=0, bytes_accessed=sum(2 * a.size * a.dtype.itemsize for a in arrays)
        ),
    )


def project_kernel(sizes, token_ref, weight_ref, *rest):
    kv_parts, per_member, half = sizes
    packets = rest[:kv_parts]
    heads_ref, away_ref = rest[kv_parts:]
    scale = math.log2(math.e) / math.sqrt(HD)
    tops, sums = [], []
    for p in packets:
        stat = p[:, per_member * HD :].astype(F32)
        whole = stat + pltpu.roll(stat, HD - TERM, 1) + pltpu.roll(stat, HD - 2 * TERM, 1)
        tops.append(whole)
        sums.append(pltpu.roll(whole, HD - SUMS, 1))
    highest = functools.reduce(jnp.maximum, tops)
    factors = [jnp.exp2((top - highest) * scale) for top in tops]
    total_sum = functools.reduce(jnp.add, [f * v for f, v in zip(factors, sums)])
    factors = [f / total_sum for f in factors]
    for i in range(per_member):
        total = 0.0
        for p, f in zip(packets, factors):
            total = total + p[:, i * HD : (i + 1) * HD].astype(F32) * f[:, i : i + 1]
        heads_ref[:, i * HD : (i + 1) * HD] = total.astype(BF16)
    part_kernel(False, heads_ref, weight_ref, away_ref)


def part_kernel(mine, heads_ref, weight_ref, out_ref):
    half = out_ref.shape[1]
    section = lax.axis_index("side")
    cols = pl.ds(pl.multiple_of((1 - section if mine else section) * half, half), half)
    out_ref[...] = jnp.dot(
        heads_ref[...], weight_ref[:, cols], preferred_element_type=F32
    ).astype(out_ref.dtype)


def add_kernel(kept_ref, came_ref, out_ref):
    out_ref[...] = (kept_ref[...] + came_ref[...].astype(F32)).astype(BF16)


def middle_kernel(half, token_ref, resid_ref, lanes_ref, *rest):
    *parts, out_ref = rest
    cols = pl.ds(pl.multiple_of(lax.axis_index("side") * half, half), half)
    total = parts[0][...].astype(F32)
    for part in parts[1:]:
        total = total + part[...].astype(F32)
    out_ref[:, :half] = (resid_ref[:, cols].astype(F32) + total).astype(BF16)
    out_ref[:, half:] = lanes_ref[...]


def scaled_rows(packets, gain_ref, side, half):
    x = jnp.concatenate([p[:, :half].astype(F32) for p in packets], axis=0)
    gain = gain_ref[:, pl.ds(pl.multiple_of(side * half, half), half)]
    return (x * gain).astype(BF16), jnp.sum(x * x, axis=1, keepdims=True)


def first_half_kernel(tile, half, gain_ref, w_ref, *rest):
    *packets, hidden_ref, square_ref, gate_ref = rest
    section = lax.axis_index("side")
    me = lax.axis_index("grp")
    x, square = scaled_rows(packets, gain_ref, 1 - section, half)
    square_ref[...] = jnp.broadcast_to(square, square_ref.shape)
    lanes = jnp.concatenate([p[:, half:].astype(F32) for p in packets], axis=0)
    lane = lax.broadcasted_iota(jnp.int32, lanes.shape, 1)
    gate = jnp.sum(jnp.where(lane % (HD // 2) == me, lanes, 0.0), axis=1, keepdims=True)
    gate_ref[...] = jnp.broadcast_to(gate, gate_ref.shape)
    rows = pl.ds(pl.multiple_of((1 - section) * half, half), half)

    def column(j, carry):
        cols = pl.ds(j * tile, tile)
        hidden_ref[:, cols] = jnp.dot(x, w_ref[0, rows, cols], preferred_element_type=F32)
        return carry

    for j in range(hidden_ref.shape[1] // tile):
        column(j, 0)


def second_half_kernel(
    tile, half, gain_ref, w_ref, hidden_ref, square_ref, gate_ref, down_ref, *rest
):
    *packets, act_ref, away_ref = rest
    inner = act_ref.shape[1]
    section = lax.axis_index("side")
    x, square = scaled_rows(packets, gain_ref, section, half)
    square = square + square_ref[:, :1]
    inv = lax.rsqrt(square / (half * lax.axis_size("side")) + 1e-6)
    rows = pl.ds(pl.multiple_of(section * half, half), half)

    def column(j, carry):
        both = []
        for base in (0, inner):
            cols = pl.ds(base + j * tile, tile)
            part = jnp.dot(x, w_ref[0, rows, cols], preferred_element_type=F32)
            both.append((hidden_ref[:, cols] + part) * inv)
        act = both[0] / (1.0 + jnp.exp(-both[0])) * both[1]
        act_ref[:, pl.ds(j * tile, tile)] = act.astype(BF16)
        return carry

    for j in range(inner // tile):
        column(j, 0)
    down(tile, act_ref, gate_ref, down_ref, away_ref, (1 - section) * half)


def down(tile, act_ref, gate_ref, down_ref, out_ref, start):
    gate = gate_ref[:, :1]
    for j in range(out_ref.shape[1] // tile):
        at = pl.ds(pl.multiple_of(start + j * tile, HD), tile)
        part = jnp.dot(act_ref[...], down_ref[0, :, at], preferred_element_type=F32)
        out_ref[:, j * tile : (j + 1) * tile] = (part * gate).astype(out_ref.dtype)


def away_kernel(tile, half, first, act_ref, gate_ref, down_ref, out_ref):
    start = (1 - lax.axis_index("side")) * half + first
    down(tile, act_ref, gate_ref, down_ref, out_ref, start)


def keep_kernel(tile, act_ref, gate_ref, down_ref, kept_ref):
    start = lax.axis_index("side") * kept_ref.shape[1]
    down(tile, act_ref, gate_ref, down_ref, kept_ref, start)


def fold_kernel(rows, kept_ref, came_ref, *sends):
    total = kept_ref[...] + came_ref[...].astype(F32)
    for b, ref in enumerate(sends):
        ref[...] = total[b * rows : (b + 1) * rows].astype(BF16)


def split_kernel(count, *refs):
    parts, sends = refs[:count], refs[count:]
    piece = sends[0].shape[1]
    me = lax.axis_index("tp")
    for mask, ref in enumerate(sends):
        at = pl.ds(pl.multiple_of((me ^ mask) * piece, piece), piece)
        total = parts[0][:, at].astype(F32)
        for part in parts[1:]:
            total = total + part[:, at].astype(F32)
        ref[...] = total.astype(BF16)


def final_kernel(middle_ref, *rest):
    *parts, out_ref = rest
    piece = out_ref.shape[1]
    at = pl.ds(pl.multiple_of(lax.axis_index("tp") * piece, piece), piece)
    total = middle_ref[:, at].astype(F32)
    for part in parts:
        total = total + part[...].astype(F32)
    out_ref[...] = total.astype(BF16)


def body(
    queries,
    kv_cache,
    lengths,
    out_weight,
    resid,
    norm_gain,
    expert_ids,
    expert_gates,
    w_gate_up,
    w_down,
):
    tp = lax.axis_size("tp")
    grp = lax.axis_size("grp")
    sides = lax.axis_size("side")
    group_size = sides * tp
    kv_parts = group_size // KVH
    group_heads = QH // KVH
    per_member = QH // group_size
    span = kv_cache.shape[2]
    width = out_weight.shape[1]
    half = width // sides
    piece = width // group_size
    rows, top = expert_ids.shape
    inner = w_down.shape[1]
    packet = (rows, (per_member + 1) * HD)
    sizes = (tp, grp, sides, kv_parts, group_heads, per_member, rows, span, top)
    many = rows * group_heads
    results = call(
        functools.partial(attention_kernel, sizes),
        [
            queries,
            lengths,
            expert_ids.T,
            expert_gates.T,
            kv_cache,
        ],
        [(packet, F32)] + [(packet, BF16)] * (kv_parts - 1)
        + [((rows, HD), BF16)],
        [
            pltpu.VMEM((rows, span, 2 * HD), BF16),
            pltpu.VMEM((rows, group_heads * HD), BF16),
            pltpu.SMEM((rows,), jnp.int32),
            pltpu.VMEM((top, rows), jnp.int32),
            pltpu.VMEM((top, rows), F32),
            pltpu.VMEM((HD, HD), F32),
            pltpu.VMEM((many, HD), F32),
            pltpu.VMEM((many, span), F32),
            pltpu.VMEM((many + group_heads, HD), F32),
            pltpu.VMEM((many + group_heads, HD), F32),
            pltpu.VMEM((many + group_heads, HD), F32),
            pltpu.SemaphoreType.DMA((3 + len(CUTS),)),
        ],
        far=range(5),
        limit=16,
        name="attention",
    )
    own, *rest = results[:kv_parts]
    gate_lanes = results[kv_parts]
    out_weight, resid, gain, token = fetched(
        gate_lanes, out_weight, resid, norm_gain.reshape(1, width)
    )
    came = [swapped(rest[mask - 1], "tp", mask) for mask in range(1, kv_parts)]
    heads, away = call(
        functools.partial(project_kernel, (kv_parts, per_member, half)),
        [token, out_weight, own, *came],
        [((rows, per_member * HD), BF16), ((rows, half), BF16)],
        name="project",
    )
    away = swapped(away, "side", 1)
    kept = call(
        functools.partial(part_kernel, True), [heads, out_weight], [((rows, half), F32)], name="kept"
    )[0]
    outgoing = call(add_kernel, [kept, away], [((rows, half), BF16)], name="pair")[0]
    w_gate_up, token = fetched(outgoing, w_gate_up)
    parts = [crossed(outgoing, 0, mask) for mask in range(tp)]
    middle = call(
        functools.partial(middle_kernel, half),
        [token, resid, gate_lanes, *parts],
        [((rows, half + HD), BF16)],
        name="middle",
    )[0]
    packets = [crossed(middle, mask) for mask in [*range(1, grp), 0]]
    packets = [packets[-1], *packets[:-1]]
    near_packets = [middle] + [swapped(p, "side", 1) for p in packets[1:]]
    total = grp * rows
    tile = 256
    hidden, square, gate = call(
        functools.partial(first_half_kernel, tile, half),
        [gain, w_gate_up, *packets],
        [((total, 2 * inner), F32), ((total, HD), F32), ((total, HD), F32)],
        name="first_half",
    )
    act, sent = call(
        functools.partial(second_half_kernel, tile, half),
        [gain, w_gate_up, hidden, square, gate, w_down, *near_packets],
        [((total, inner), BF16), ((total, half), BF16)],
        name="second_half",
    )
    back = swapped(sent, "side", 1)
    mine = call(
        functools.partial(keep_kernel, tile),
        [act, gate, w_down],
        [((total, half), F32)],
        name="keep",
    )[0]
    sends = call(
        functools.partial(fold_kernel, rows),
        [mine, back],
        [((rows, half), BF16)] * grp,
        name="fold",
    )
    came = [crossed(sends[mask], mask) for mask in reversed(range(grp))]
    sends = call(
        functools.partial(split_kernel, grp),
        came,
        [((rows, piece), BF16)] * tp,
        name="split",
    )
    came = [crossed(sends[mask], 0, mask) for mask in reversed(range(tp))]
    ins = [middle, *came]
    return pl.pallas_call(
        final_kernel,
        out_shape=jax.ShapeDtypeStruct((rows, piece), BF16),
        in_specs=[VMEM_SPEC] * len(ins),
        out_specs=VMEM_SPEC,
        name="final",
    )(*map(near, ins))


def solution(mesh):
    in_specs = (
        P("grp", "side"),
        P("grp", ("side", "tp"), None, None),
        P("grp"),
        P(("side", "tp"), None),
        P("grp", None),
        P(),
        P("grp", None),
        P("grp", None),
        P(("side", "grp", "tp"), None, None),
        P(("side", "grp", "tp"), None, None),
    )
    out_specs = P("grp", ("side", "tp"))
    return jax.shard_map(body, mesh=mesh, in_specs=in_specs, out_specs=out_specs, check_vma=False)
```

```python
import functools
import math

import jax
import jax.numpy as jnp
from jax import lax
from jax.experimental import pallas as pl
from jax.experimental.pallas import tpu as pltpu
from jax.sharding import PartitionSpec as P

QH = 32
KVH = 4
HD = 128
LOW = -1e30
SUMS = 16
TERM = 32
CUTS = (0, 6, 12, 18, 24)
CUT_OF = 24
LAG = 2
F32 = jnp.float32
BF16 = jnp.bfloat16
MIB = 1024 * 1024
VMEM_SPEC = pl.BlockSpec(memory_space=pltpu.VMEM)


def swapped(value, axis, mask):
    pairs = [(source, source ^ mask) for source in range(lax.axis_size(axis))]
    return lax.ppermute(value, axis, pairs)


def crossed(value, mask, along=0):
    grp, tp = lax.axis_size("grp"), lax.axis_size("tp")
    pairs = [
        ((s * grp + g) * tp + t, ((1 - s) * grp + (g ^ mask)) * tp + (t ^ along))
        for s in range(2)
        for g in range(grp)
        for t in range(tp)
    ]
    return lax.ppermute(value, ("side", "grp", "tp"), pairs)


def near(value, space=pltpu.VMEM):
    return pltpu.with_memory_space_constraint(value, space)


def call(kernel, ins, outs, scratch=(), far=(), limit=8, name=None, cost=None):
    spaces = [pltpu.HBM if i in far else pltpu.VMEM for i in range(len(ins))]
    return pl.pallas_call(
        kernel,
        out_shape=[pltpu.VMEM(shape, dtype) for shape, dtype in outs],
        in_specs=[pl.BlockSpec(memory_space=s) for s in spaces],
        out_specs=[VMEM_SPEC] * len(outs),
        scratch_shapes=list(scratch),
        compiler_params=pltpu.CompilerParams(vmem_limit_bytes=limit * MIB),
        name=name,
        cost_estimate=cost,
    )(*[near(a, s) for a, s in zip(ins, spaces)])


def attention_kernel(sizes, *refs):
    tp, grp, sides, kv_parts, group_heads, per_member, rows, span, top = sizes
    q_hbm, len_hbm, ids_hbm, gates_hbm, kv_hbm = refs[:5]
    own_ref, *send_refs = refs[5 : 5 + kv_parts]
    lanes_ref = refs[5 + kv_parts]
    kv, q_in, len_ref, ids_ref, gates_ref, q_s, score_s, num_s, max_s, sum_s, sems = refs[
        6 + kv_parts :
    ]
    cuts = [rows * c // CUT_OF for c in CUTS]
    chunks = list(zip(cuts, cuts[1:]))
    section = lax.axis_index("side")
    tp_index = lax.axis_index("tp")
    part = tp_index % kv_parts
    q_cols = pl.ds(
        pl.multiple_of(tp_index // kv_parts * (group_heads * HD), group_heads * HD), group_heads * HD
    )
    pairs = [
        (q_hbm.at[:, q_cols], q_in),
        (len_hbm, len_ref),
        (ids_hbm, ids_ref),
        (gates_hbm, gates_ref),
        *[(kv_hbm.at[pl.ds(a, b - a), 0], kv.at[pl.ds(a, b - a)]) for a, b in chunks],
    ]
    copies = [pltpu.make_async_copy(a, b, sems.at[i]) for i, (a, b) in enumerate(pairs)]
    for copy in copies:
        copy.start()
    for copy in copies[:4]:
        copy.wait()
    for g in range(group_heads):
        q_s[pl.ds(g, rows, stride=group_heads), :] = q_in[:, g * HD : (g + 1) * HD].astype(F32)
    place = lax.broadcasted_iota(jnp.int32, (2 * grp, rows), 0)
    expert = ((1 - section) * grp + place % grp) * tp + tp_index
    gate = jnp.zeros((2 * grp, rows), F32)
    for k in range(top):
        gate = gate + jnp.where(ids_ref[k : k + 1, :] == expert, gates_ref[k : k + 1, :], 0.0)
    high = gate.astype(BF16).astype(F32)
    lanes_ref[...] = jnp.zeros(lanes_ref.shape, F32)
    lanes_ref[:, :rows] = jnp.where(place < grp, high, gate - high)
    scale = math.log2(math.e) / math.sqrt(HD)
    place = part * span + lax.broadcasted_iota(jnp.int32, (group_heads, span), 1)
    def spot(r):
        return pl.ds(r * group_heads, group_heads)

    def values(some):
        for r in some:
            valid = place < len_ref[r]
            score = jnp.where(valid, score_s[spot(r), :], LOW)
            top_score = jnp.max(score, axis=-1, keepdims=True)
            weight = jnp.where(valid, jnp.exp2((score - top_score) * scale), 0.0)
            max_s[spot(r), :] = jnp.broadcast_to(top_score, (group_heads, HD))
            sum_s[spot(r), :] = jnp.broadcast_to(
                jnp.sum(weight, axis=-1, keepdims=True), (group_heads, HD)
            )
            num_s[spot(r), :] = jnp.dot(
                weight.astype(BF16), kv[r, :, HD:], preferred_element_type=F32
            )

    for c, span_of in enumerate(chunks):
        copies[4 + c].wait()
        for r in range(span_of[0], span_of[1], 2):
            both = pl.ds(r * group_heads, 2 * group_heads)
            q = q_s[both, :]
            upper = lax.broadcasted_iota(jnp.int32, q.shape, 0) < group_heads
            q = jnp.concatenate([jnp.where(upper, q, 0.0), jnp.where(upper, 0.0, q)], axis=1)
            score_s[both, :] = lax.dot_general(
                q.astype(BF16),
                jnp.concatenate([kv[r, :, :HD], kv[r + 1, :, :HD]], axis=1),
                (((1,), (1,)), ((), ())),
                preferred_element_type=F32,
            )
        if c >= LAG:
            values(range(*chunks[c - LAG]))
    values(range(cuts[-1 - LAG], rows))
    lane = lax.broadcasted_iota(jnp.int32, (rows, HD), 1)
    for mask, out in enumerate([own_ref, *send_refs]):
        first = (part ^ mask) * per_member
        stats = jnp.zeros((rows, HD), F32)
        for i in range(per_member):
            pick = pl.ds(first + i, rows, stride=group_heads)
            out[:, i * HD : (i + 1) * HD] = num_s[pick, :].astype(out.dtype)
            stats = jnp.where(lane == i, max_s[pick, :], stats)
            stats = jnp.where(lane == SUMS + i, sum_s[pick, :], stats)
        sent = jnp.zeros((rows, HD), F32)
        for k in range(3):
            term = stats.astype(out.dtype).astype(F32)
            sent = sent + (pltpu.roll(term, k * TERM, 1) if k else term)
            stats = stats - term
        out[:, per_member * HD :] = sent.astype(out.dtype)


def fetch_kernel(parts, after_ref, *refs):
    count = (len(refs) - 2) // 2
    sources, targets, token_ref, sems = refs[:count], refs[count:-2], refs[-2], refs[-1]
    copies = []
    for source, target, number in zip(sources, targets, parts):
        axis = source.ndim - 2
        step = source.shape[axis] // number
        for j in range(number):
            at = (slice(None),) * axis + (pl.ds(j * step, step),)
            copies.append(
                pltpu.make_async_copy(source.at[at], target.at[at], sems.at[len(copies)])
            )
            copies[-1].start()
    token_ref[...] = after_ref[:, :HD]
    for copy in copies:
        copy.wait()


def fetched(after, *arrays):
    rows = after.shape[0]
    parts = [4 if a.size > MIB // 2 else 1 for a in arrays]
    return call(
        functools.partial(fetch_kernel, parts),
        [after, *arrays],
        [(a.shape, a.dtype) for a in arrays] + [((rows, HD), after.dtype)],
        [pltpu.SemaphoreType.DMA((sum(parts),))],
        far=range(1, len(arrays) + 1),
        name="fetch",
        cost=pl.CostEstimate(
            flops=0, transcendentals=0, bytes_accessed=sum(2 * a.size * a.dtype.itemsize for a in arrays)
        ),
    )


def project_kernel(sizes, token_ref, weight_ref, *rest):
    kv_parts, per_member, half = sizes
    packets = rest[:kv_parts]
    heads_ref, away_ref = rest[kv_parts:]
    scale = math.log2(math.e) / math.sqrt(HD)
    tops, sums = [], []
    for p in packets:
        stat = p[:, per_member * HD :].astype(F32)
        whole = stat + pltpu.roll(stat, HD - TERM, 1) + pltpu.roll(stat, HD - 2 * TERM, 1)
        tops.append(whole)
        sums.append(pltpu.roll(whole, HD - SUMS, 1))
    highest = functools.reduce(jnp.maximum, tops)
    factors = [jnp.exp2((top - highest) * scale) for top in tops]
    total_sum = functools.reduce(jnp.add, [f * v for f, v in zip(factors, sums)])
    factors = [f / total_sum for f in factors]
    for i in range(per_member):
        total = 0.0
        for p, f in zip(packets, factors):
            total = total + p[:, i * HD : (i + 1) * HD].astype(F32) * f[:, i : i + 1]
        heads_ref[:, i * HD : (i + 1) * HD] = total.astype(BF16)
    part_kernel(False, heads_ref, weight_ref, away_ref)


def part_kernel(mine, heads_ref, weight_ref, out_ref):
    half = out_ref.shape[1]
    section = lax.axis_index("side")
    cols = pl.ds(pl.multiple_of((1 - section if mine else section) * half, half), half)
    out_ref[...] = jnp.dot(
        heads_ref[...], weight_ref[:, cols], preferred_element_type=F32
    ).astype(out_ref.dtype)


def add_kernel(kept_ref, came_ref, out_ref):
    out_ref[...] = (kept_ref[...] + came_ref[...].astype(F32)).astype(BF16)


def middle_kernel(half, token_ref, resid_ref, lanes_ref, *rest):
    *parts, middle_ref, packet_ref = rest
    cols = pl.ds(pl.multiple_of(lax.axis_index("side") * half, half), half)
    total = parts[0][...].astype(F32)
    for part in parts[1:]:
        total = total + part[...].astype(F32)
    middle = (resid_ref[:, cols].astype(F32) + total).astype(BF16)
    middle_ref[...] = middle
    middle = middle.astype(F32)
    blocks = [middle[:, c : c + HD] for c in range(0, half, HD)]
    packet_ref[...] = jnp.concatenate([*blocks, lanes_ref[...]], axis=0).astype(BF16)


def packet_rows(packet, rows, half):
    packet = packet[...].astype(F32)
    return jnp.concatenate([packet[c * rows : (c + 1) * rows] for c in range(half // HD)], axis=1)


def scaled_rows(packets, rows, gain_ref, side, half):
    x = jnp.concatenate([packet_rows(p, rows, half) for p in packets], axis=0)
    gain = gain_ref[:, pl.ds(pl.multiple_of(side * half, half), half)]
    return (x * gain).astype(BF16), jnp.sum(x * x, axis=1, keepdims=True)


def first_half_kernel(tile, rows, half, gain_ref, w_ref, *rest):
    *packets, hidden_ref, square_ref, gate_ref = rest
    section = lax.axis_index("side")
    me = lax.axis_index("grp")
    x, square = scaled_rows(packets, rows, gain_ref, 1 - section, half)
    square_ref[...] = jnp.broadcast_to(square, square_ref.shape)
    for b, packet in enumerate(packets):
        lanes = packet[...].astype(F32)[half // HD * rows :]
        row = lax.broadcasted_iota(jnp.int32, lanes.shape, 0)
        groups = lanes.shape[0] // 2
        gate = jnp.sum(jnp.where(row % groups == me, lanes, 0.0), axis=0, keepdims=True)
        gate_ref[b * rows : (b + 1) * rows, :] = jnp.broadcast_to(gate, (HD, HD)).T[:rows]
    depth = pl.ds(pl.multiple_of((1 - section) * half, half), half)

    def column(j, carry):
        cols = pl.ds(j * tile, tile)
        hidden_ref[:, cols] = jnp.dot(x, w_ref[0, depth, cols], preferred_element_type=F32)
        return carry

    for j in range(hidden_ref.shape[1] // tile):
        column(j, 0)


def second_half_kernel(
    tile, rows, half, gain_ref, w_ref, hidden_ref, square_ref, gate_ref, down_ref, *rest
):
    *packets, act_ref, away_ref = rest
    inner = act_ref.shape[1]
    section = lax.axis_index("side")
    x, square = scaled_rows(packets, rows, gain_ref, section, half)
    square = square + square_ref[:, :1]
    inv = lax.rsqrt(square / (half * lax.axis_size("side")) + 1e-6)
    depth = pl.ds(pl.multiple_of(section * half, half), half)

    def column(j, carry):
        both = []
        for base in (0, inner):
            cols = pl.ds(base + j * tile, tile)
            part = jnp.dot(x, w_ref[0, depth, cols], preferred_element_type=F32)
            both.append((hidden_ref[:, cols] + part) * inv)
        act = both[0] / (1.0 + jnp.exp(-both[0])) * both[1]
        act_ref[:, pl.ds(j * tile, tile)] = act.astype(BF16)
        return carry

    for j in range(inner // tile):
        column(j, 0)
    down(tile, act_ref, gate_ref, down_ref, away_ref, (1 - section) * half)


def down(tile, act_ref, gate_ref, down_ref, out_ref, start):
    gate = gate_ref[:, :1]
    for j in range(out_ref.shape[1] // tile):
        at = pl.ds(pl.multiple_of(start + j * tile, HD), tile)
        part = jnp.dot(act_ref[...], down_ref[0, :, at], preferred_element_type=F32)
        out_ref[:, j * tile : (j + 1) * tile] = (part * gate).astype(out_ref.dtype)


def away_kernel(tile, half, first, act_ref, gate_ref, down_ref, out_ref):
    start = (1 - lax.axis_index("side")) * half + first
    down(tile, act_ref, gate_ref, down_ref, out_ref, start)


def keep_kernel(tile, act_ref, gate_ref, down_ref, kept_ref):
    start = lax.axis_index("side") * kept_ref.shape[1]
    down(tile, act_ref, gate_ref, down_ref, kept_ref, start)


def fold_kernel(rows, kept_ref, came_ref, *sends):
    total = kept_ref[...] + came_ref[...].astype(F32)
    for b, ref in enumerate(sends):
        ref[...] = total[b * rows : (b + 1) * rows].astype(BF16)


def split_kernel(count, *refs):
    parts, sends = refs[:count], refs[count:]
    piece = sends[0].shape[1]
    me = lax.axis_index("tp")
    for mask, ref in enumerate(sends):
        at = pl.ds(pl.multiple_of((me ^ mask) * piece, piece), piece)
        total = parts[0][:, at].astype(F32)
        for part in parts[1:]:
            total = total + part[:, at].astype(F32)
        ref[...] = total.astype(BF16)


def final_kernel(middle_ref, *rest):
    *parts, out_ref = rest
    piece = out_ref.shape[1]
    at = pl.ds(pl.multiple_of(lax.axis_index("tp") * piece, piece), piece)
    total = middle_ref[:, at].astype(F32)
    for part in parts:
        total = total + part[...].astype(F32)
    out_ref[...] = total.astype(BF16)


def body(
    queries,
    kv_cache,
    lengths,
    out_weight,
    resid,
    norm_gain,
    expert_ids,
    expert_gates,
    w_gate_up,
    w_down,
):
    tp = lax.axis_size("tp")
    grp = lax.axis_size("grp")
    sides = lax.axis_size("side")
    group_size = sides * tp
    kv_parts = group_size // KVH
    group_heads = QH // KVH
    per_member = QH // group_size
    span = kv_cache.shape[2]
    width = out_weight.shape[1]
    half = width // sides
    piece = width // group_size
    rows, top = expert_ids.shape
    inner = w_down.shape[1]
    partial_shape = (rows, (per_member + 1) * HD)
    sizes = (tp, grp, sides, kv_parts, group_heads, per_member, rows, span, top)
    many = rows * group_heads
    results = call(
        functools.partial(attention_kernel, sizes),
        [
            queries,
            lengths,
            expert_ids.T,
            expert_gates.T,
            kv_cache,
        ],
        [(partial_shape, F32)] + [(partial_shape, BF16)] * (kv_parts - 1)
        + [((2 * grp, HD), F32)],
        [
            pltpu.VMEM((rows, span, 2 * HD), BF16),
            pltpu.VMEM((rows, group_heads * HD), BF16),
            pltpu.SMEM((rows,), jnp.int32),
            pltpu.VMEM((top, rows), jnp.int32),
            pltpu.VMEM((top, rows), F32),
            pltpu.VMEM((many, HD), F32),
            pltpu.VMEM((many, span), F32),
            pltpu.VMEM((many + group_heads, HD), F32),
            pltpu.VMEM((many + group_heads, HD), F32),
            pltpu.VMEM((many + group_heads, HD), F32),
            pltpu.SemaphoreType.DMA((3 + len(CUTS),)),
        ],
        far=range(5),
        limit=16,
        name="attention",
    )
    own, *rest = results[:kv_parts]
    gate_lanes = results[kv_parts]
    out_weight, resid, gain, token = fetched(
        gate_lanes, out_weight, resid, norm_gain.reshape(1, width)
    )
    came = [swapped(rest[mask - 1], "tp", mask) for mask in range(1, kv_parts)]
    heads, away = call(
        functools.partial(project_kernel, (kv_parts, per_member, half)),
        [token, out_weight, own, *came],
        [((rows, per_member * HD), BF16), ((rows, half), BF16)],
        name="project",
    )
    away = swapped(away, "side", 1)
    kept = call(
        functools.partial(part_kernel, True), [heads, out_weight], [((rows, half), F32)], name="kept"
    )[0]
    outgoing = call(add_kernel, [kept, away], [((rows, half), BF16)], name="pair")[0]
    w_gate_up, token = fetched(outgoing, w_gate_up)
    parts = [crossed(outgoing, 0, mask) for mask in range(tp)]
    middle, packet = call(
        functools.partial(middle_kernel, half),
        [token, resid, gate_lanes, *parts],
        [((rows, half), BF16), ((half // HD * rows + 2 * grp, HD), BF16)],
        name="middle",
    )
    packets = [crossed(packet, mask) for mask in [*range(1, grp), 0]]
    packets = [packets[-1], *packets[:-1]]
    near_packets = [packet] + [swapped(p, "side", 1) for p in packets[1:]]
    total = grp * rows
    tile = 256
    hidden, square, gate = call(
        functools.partial(first_half_kernel, tile, rows, half),
        [gain, w_gate_up, *packets],
        [((total, 2 * inner), F32), ((total, HD), F32), ((total, HD), F32)],
        name="first_half",
    )
    act, sent = call(
        functools.partial(second_half_kernel, tile, rows, half),
        [gain, w_gate_up, hidden, square, gate, w_down, *near_packets],
        [((total, inner), BF16), ((total, half), BF16)],
        name="second_half",
    )
    back = swapped(sent, "side", 1)
    mine = call(
        functools.partial(keep_kernel, tile),
        [act, gate, w_down],
        [((total, half), F32)],
        name="keep",
    )[0]
    sends = call(
        functools.partial(fold_kernel, rows),
        [mine, back],
        [((rows, half), BF16)] * grp,
        name="fold",
    )
    came = [crossed(sends[mask], mask) for mask in reversed(range(grp))]
    sends = call(
        functools.partial(split_kernel, grp),
        came,
        [((rows, piece), BF16)] * tp,
        name="split",
    )
    came = [crossed(sends[mask], 0, mask) for mask in reversed(range(tp))]
    ins = [middle, *came]
    return pl.pallas_call(
        final_kernel,
        out_shape=jax.ShapeDtypeStruct((rows, piece), BF16),
        in_specs=[VMEM_SPEC] * len(ins),
        out_specs=VMEM_SPEC,
        name="final",
    )(*map(near, ins))


def solution(mesh):
    in_specs = (
        P("grp", "side"),
        P("grp", ("side", "tp"), None, None),
        P("grp"),
        P(("side", "tp"), None),
        P("grp", None),
        P(),
        P("grp", None),
        P("grp", None),
        P(("side", "grp", "tp"), None, None),
        P(("side", "grp", "tp"), None, None),
    )
    out_specs = P("grp", ("side", "tp"))
    return jax.shard_map(body, mesh=mesh, in_specs=in_specs, out_specs=out_specs, check_vma=False)
```

```python
import functools
import math

import jax
import jax.numpy as jnp
from jax import lax
from jax.experimental import pallas as pl
from jax.experimental.pallas import tpu as pltpu
from jax.sharding import PartitionSpec as P

QH = 32
KVH = 4
HD = 128
LOW = -1e30
SUMS = 16
TERM = 32
CUTS = (0, 6, 12, 18, 24)
CUT_OF = 24
LAG = 2
F32 = jnp.float32
BF16 = jnp.bfloat16
MIB = 1024 * 1024
VMEM_SPEC = pl.BlockSpec(memory_space=pltpu.VMEM)


def swapped(value, axis, mask):
    pairs = [(source, source ^ mask) for source in range(lax.axis_size(axis))]
    return lax.ppermute(value, axis, pairs)


def crossed(value, mask, along=0):
    grp, tp = lax.axis_size("grp"), lax.axis_size("tp")
    pairs = [
        ((s * grp + g) * tp + t, ((1 - s) * grp + (g ^ mask)) * tp + (t ^ along))
        for s in range(2)
        for g in range(grp)
        for t in range(tp)
    ]
    return lax.ppermute(value, ("side", "grp", "tp"), pairs)


def near(value, space=pltpu.VMEM):
    return pltpu.with_memory_space_constraint(value, space)


def call(kernel, ins, outs, scratch=(), far=(), limit=8, name=None, cost=None):
    spaces = [pltpu.HBM if i in far else pltpu.VMEM for i in range(len(ins))]
    return pl.pallas_call(
        kernel,
        out_shape=[pltpu.VMEM(shape, dtype) for shape, dtype in outs],
        in_specs=[pl.BlockSpec(memory_space=s) for s in spaces],
        out_specs=[VMEM_SPEC] * len(outs),
        scratch_shapes=list(scratch),
        compiler_params=pltpu.CompilerParams(vmem_limit_bytes=limit * MIB),
        name=name,
        cost_estimate=cost,
    )(*[near(a, s) for a, s in zip(ins, spaces)])


def attention_kernel(sizes, *refs):
    tp, grp, sides, kv_parts, group_heads, per_member, rows, span, top = sizes
    q_hbm, len_hbm, ids_hbm, gates_hbm, kv_hbm = refs[:5]
    own_ref, *send_refs = refs[5 : 5 + kv_parts]
    lanes_ref = refs[5 + kv_parts]
    kv, q_in, len_ref, ids_ref, gates_ref, q_s, score_s, num_s, max_s, sum_s, sems = refs[
        6 + kv_parts :
    ]
    cuts = [rows * c // CUT_OF for c in CUTS]
    chunks = list(zip(cuts, cuts[1:]))
    section = lax.axis_index("side")
    tp_index = lax.axis_index("tp")
    part = tp_index % kv_parts
    q_cols = pl.ds(
        pl.multiple_of(tp_index // kv_parts * (group_heads * HD), group_heads * HD), group_heads * HD
    )
    pairs = [
        (q_hbm.at[:, q_cols], q_in),
        (len_hbm, len_ref),
        (ids_hbm, ids_ref),
        (gates_hbm, gates_ref),
        *[(kv_hbm.at[pl.ds(a, b - a), 0], kv.at[pl.ds(a, b - a)]) for a, b in chunks],
    ]
    copies = [pltpu.make_async_copy(a, b, sems.at[i]) for i, (a, b) in enumerate(pairs)]
    for copy in copies:
        copy.start()
    for copy in copies[:4]:
        copy.wait()
    for g in range(group_heads):
        q_s[pl.ds(g, rows, stride=group_heads), :] = q_in[:, g * HD : (g + 1) * HD].astype(F32)
    place = lax.broadcasted_iota(jnp.int32, (2 * grp, rows), 0)
    expert = ((1 - section) * grp + place % grp) * tp + tp_index
    gate = jnp.zeros((2 * grp, rows), F32)
    for k in range(top):
        gate = gate + jnp.where(ids_ref[k : k + 1, :] == expert, gates_ref[k : k + 1, :], 0.0)
    high = gate.astype(BF16).astype(F32)
    lanes_ref[...] = jnp.zeros(lanes_ref.shape, F32)
    lanes_ref[:, :rows] = jnp.where(place < grp, high, gate - high)
    scale = math.log2(math.e) / math.sqrt(HD)
    place = part * span + lax.broadcasted_iota(jnp.int32, (group_heads, span), 1)
    def spot(r):
        return pl.ds(r * group_heads, group_heads)

    def values(some):
        for r in some:
            valid = place < len_ref[r]
            score = jnp.where(valid, score_s[spot(r), :], LOW)
            top_score = jnp.max(score, axis=-1, keepdims=True)
            weight = jnp.where(valid, jnp.exp2((score - top_score) * scale), 0.0)
            max_s[spot(r), :] = jnp.broadcast_to(top_score, (group_heads, HD))
            sum_s[spot(r), :] = jnp.broadcast_to(
                jnp.sum(weight, axis=-1, keepdims=True), (group_heads, HD)
            )
            num_s[spot(r), :] = jnp.dot(
                weight.astype(BF16), kv[r, :, HD:], preferred_element_type=F32
            )

    for c, span_of in enumerate(chunks):
        copies[4 + c].wait()
        for r in range(span_of[0], span_of[1], 2):
            both = pl.ds(r * group_heads, 2 * group_heads)
            q = q_s[both, :]
            upper = lax.broadcasted_iota(jnp.int32, q.shape, 0) < group_heads
            q = jnp.concatenate([jnp.where(upper, q, 0.0), jnp.where(upper, 0.0, q)], axis=1)
            score_s[both, :] = lax.dot_general(
                q.astype(BF16),
                jnp.concatenate([kv[r, :, :HD], kv[r + 1, :, :HD]], axis=1),
                (((1,), (1,)), ((), ())),
                preferred_element_type=F32,
            )
        if c >= LAG:
            values(range(*chunks[c - LAG]))
    values(range(cuts[-1 - LAG], rows))
    lane = lax.broadcasted_iota(jnp.int32, (rows, HD), 1)
    for mask, out in enumerate([own_ref, *send_refs]):
        first = (part ^ mask) * per_member
        stats = jnp.zeros((rows, HD), F32)
        for i in range(per_member):
            pick = pl.ds(first + i, rows, stride=group_heads)
            out[:, i * HD : (i + 1) * HD] = num_s[pick, :].astype(out.dtype)
            stats = jnp.where(lane == i, max_s[pick, :], stats)
            stats = jnp.where(lane == SUMS + i, sum_s[pick, :], stats)
        sent = jnp.zeros((rows, HD), F32)
        for k in range(3):
            term = stats.astype(out.dtype).astype(F32)
            sent = sent + (pltpu.roll(term, k * TERM, 1) if k else term)
            stats = stats - term
        out[:, per_member * HD :] = sent.astype(out.dtype)


def fetch_kernel(parts, after_ref, *refs):
    count = (len(refs) - 2) // 2
    sources, targets, token_ref, sems = refs[:count], refs[count:-2], refs[-2], refs[-1]
    copies = []
    for source, target, number in zip(sources, targets, parts):
        axis = source.ndim - 2
        step = source.shape[axis] // number
        for j in range(number):
            at = (slice(None),) * axis + (pl.ds(j * step, step),)
            copies.append(
                pltpu.make_async_copy(source.at[at], target.at[at], sems.at[len(copies)])
            )
            copies[-1].start()
    token_ref[...] = after_ref[:, :HD]
    for copy in copies:
        copy.wait()


def fetched(after, *arrays):
    rows = after.shape[0]
    parts = [4 if a.size > MIB // 2 else 1 for a in arrays]
    return call(
        functools.partial(fetch_kernel, parts),
        [after, *arrays],
        [(a.shape, a.dtype) for a in arrays] + [((rows, HD), after.dtype)],
        [pltpu.SemaphoreType.DMA((sum(parts),))],
        far=range(1, len(arrays) + 1),
        name="fetch",
        cost=pl.CostEstimate(
            flops=0, transcendentals=0, bytes_accessed=sum(2 * a.size * a.dtype.itemsize for a in arrays)
        ),
    )


def project_kernel(sizes, token_ref, weight_ref, *rest):
    kv_parts, per_member, half = sizes
    packets = rest[:kv_parts]
    heads_ref, away_ref = rest[kv_parts:]
    scale = math.log2(math.e) / math.sqrt(HD)
    tops, sums = [], []
    for p in packets:
        stat = p[:, per_member * HD :].astype(F32)
        whole = stat + pltpu.roll(stat, HD - TERM, 1) + pltpu.roll(stat, HD - 2 * TERM, 1)
        tops.append(whole)
        sums.append(pltpu.roll(whole, HD - SUMS, 1))
    highest = functools.reduce(jnp.maximum, tops)
    factors = [jnp.exp2((top - highest) * scale) for top in tops]
    total_sum = functools.reduce(jnp.add, [f * v for f, v in zip(factors, sums)])
    factors = [f / total_sum for f in factors]
    section = lax.axis_index("side")
    cols = pl.ds(pl.multiple_of(section * half, half), half)
    projected = 0.0
    for first in range(0, per_member, 2):
        pair = []
        for i in range(first, min(first + 2, per_member)):
            total = 0.0
            for p, f in zip(packets, factors):
                total = total + p[:, i * HD : (i + 1) * HD].astype(F32) * f[:, i : i + 1]
            pair.append(total.astype(BF16))
            heads_ref[:, i * HD : (i + 1) * HD] = pair[-1]
        depth = slice(first * HD, (first + len(pair)) * HD)
        projected = projected + jnp.dot(
            jnp.concatenate(pair, axis=1), weight_ref[depth, cols], preferred_element_type=F32
        )
    away_ref[...] = projected.astype(BF16)


def part_kernel(mine, heads_ref, weight_ref, out_ref):
    half = out_ref.shape[1]
    section = lax.axis_index("side")
    cols = pl.ds(pl.multiple_of((1 - section if mine else section) * half, half), half)
    out_ref[...] = jnp.dot(
        heads_ref[...], weight_ref[:, cols], preferred_element_type=F32
    ).astype(out_ref.dtype)


def add_kernel(kept_ref, came_ref, out_ref):
    out_ref[...] = (kept_ref[...] + came_ref[...].astype(F32)).astype(BF16)


def middle_kernel(half, token_ref, resid_ref, lanes_ref, *rest):
    *parts, middle_ref, packet_ref = rest
    cols = pl.ds(pl.multiple_of(lax.axis_index("side") * half, half), half)
    total = parts[0][...].astype(F32)
    for part in parts[1:]:
        total = total + part[...].astype(F32)
    middle = (resid_ref[:, cols].astype(F32) + total).astype(BF16)
    middle_ref[...] = middle
    middle = middle.astype(F32)
    blocks = [middle[:, c : c + HD] for c in range(0, half, HD)]
    packet_ref[...] = jnp.concatenate([*blocks, lanes_ref[...]], axis=0).astype(BF16)


def packet_rows(packet, rows, half):
    packet = packet[...].astype(F32)
    return jnp.concatenate([packet[c * rows : (c + 1) * rows] for c in range(half // HD)], axis=1)


def scaled_rows(packets, rows, gain_ref, side, half):
    x = jnp.concatenate([packet_rows(p, rows, half) for p in packets], axis=0)
    gain = gain_ref[:, pl.ds(pl.multiple_of(side * half, half), half)]
    return (x * gain).astype(BF16), jnp.sum(x * x, axis=1, keepdims=True)


def first_half_kernel(tile, rows, half, gain_ref, w_ref, *rest):
    *packets, hidden_ref, square_ref, gate_ref = rest
    section = lax.axis_index("side")
    me = lax.axis_index("grp")
    x, square = scaled_rows(packets, rows, gain_ref, 1 - section, half)
    square_ref[...] = jnp.broadcast_to(square, square_ref.shape)
    for b, packet in enumerate(packets):
        lanes = packet[...].astype(F32)[half // HD * rows :]
        row = lax.broadcasted_iota(jnp.int32, lanes.shape, 0)
        groups = lanes.shape[0] // 2
        gate = jnp.sum(jnp.where(row % groups == me, lanes, 0.0), axis=0, keepdims=True)
        gate_ref[b * rows : (b + 1) * rows, :] = jnp.broadcast_to(gate, (HD, HD)).T[:rows]
    depth = pl.ds(pl.multiple_of((1 - section) * half, half), half)

    def column(j, carry):
        cols = pl.ds(j * tile, tile)
        hidden_ref[:, cols] = jnp.dot(x, w_ref[0, depth, cols], preferred_element_type=F32)
        return carry

    for j in range(hidden_ref.shape[1] // tile):
        column(j, 0)


def second_half_kernel(
    tile, rows, half, gain_ref, w_ref, hidden_ref, square_ref, gate_ref, down_ref, *rest
):
    *packets, act_ref, away_ref = rest
    inner = act_ref.shape[1]
    section = lax.axis_index("side")
    x, square = scaled_rows(packets, rows, gain_ref, section, half)
    square = square + square_ref[:, :1]
    inv = lax.rsqrt(square / (half * lax.axis_size("side")) + 1e-6)
    depth = pl.ds(pl.multiple_of(section * half, half), half)

    def column(j, carry):
        both = []
        for base in (0, inner):
            cols = pl.ds(base + j * tile, tile)
            part = jnp.dot(x, w_ref[0, depth, cols], preferred_element_type=F32)
            both.append((hidden_ref[:, cols] + part) * inv)
        act = both[0] / (1.0 + jnp.exp(-both[0])) * both[1]
        act_ref[:, pl.ds(j * tile, tile)] = act.astype(BF16)
        return carry

    for j in range(inner // tile):
        column(j, 0)
    down(tile, act_ref, gate_ref, down_ref, away_ref, (1 - section) * half)


def down(tile, act_ref, gate_ref, down_ref, out_ref, start):
    gate = gate_ref[:, :1]
    for j in range(out_ref.shape[1] // tile):
        at = pl.ds(pl.multiple_of(start + j * tile, HD), tile)
        part = jnp.dot(act_ref[...], down_ref[0, :, at], preferred_element_type=F32)
        out_ref[:, j * tile : (j + 1) * tile] = (part * gate).astype(out_ref.dtype)


def away_kernel(tile, half, first, act_ref, gate_ref, down_ref, out_ref):
    start = (1 - lax.axis_index("side")) * half + first
    down(tile, act_ref, gate_ref, down_ref, out_ref, start)


def keep_kernel(tile, act_ref, gate_ref, down_ref, kept_ref):
    start = lax.axis_index("side") * kept_ref.shape[1]
    down(tile, act_ref, gate_ref, down_ref, kept_ref, start)


def fold_kernel(rows, kept_ref, came_ref, *sends):
    total = kept_ref[...] + came_ref[...].astype(F32)
    for b, ref in enumerate(sends):
        ref[...] = total[b * rows : (b + 1) * rows].astype(BF16)


def split_kernel(count, *refs):
    parts, sends = refs[:count], refs[count:]
    piece = sends[0].shape[1]
    me = lax.axis_index("tp")
    for mask, ref in enumerate(sends):
        at = pl.ds(pl.multiple_of((me ^ mask) * piece, piece), piece)
        total = parts[0][:, at].astype(F32)
        for part in parts[1:]:
            total = total + part[:, at].astype(F32)
        ref[...] = total.astype(BF16)


def final_kernel(middle_ref, *rest):
    *parts, out_ref = rest
    piece = out_ref.shape[1]
    at = pl.ds(pl.multiple_of(lax.axis_index("tp") * piece, piece), piece)
    total = middle_ref[:, at].astype(F32)
    for part in parts:
        total = total + part[...].astype(F32)
    out_ref[...] = total.astype(BF16)


def body(
    queries,
    kv_cache,
    lengths,
    out_weight,
    resid,
    norm_gain,
    expert_ids,
    expert_gates,
    w_gate_up,
    w_down,
):
    tp = lax.axis_size("tp")
    grp = lax.axis_size("grp")
    sides = lax.axis_size("side")
    group_size = sides * tp
    kv_parts = group_size // KVH
    group_heads = QH // KVH
    per_member = QH // group_size
    span = kv_cache.shape[2]
    width = out_weight.shape[1]
    half = width // sides
    piece = width // group_size
    rows, top = expert_ids.shape
    inner = w_down.shape[1]
    partial_shape = (rows, (per_member + 1) * HD)
    sizes = (tp, grp, sides, kv_parts, group_heads, per_member, rows, span, top)
    many = rows * group_heads
    results = call(
        functools.partial(attention_kernel, sizes),
        [
            queries,
            lengths,
            expert_ids.T,
            expert_gates.T,
            kv_cache,
        ],
        [(partial_shape, F32)] + [(partial_shape, BF16)] * (kv_parts - 1)
        + [((2 * grp, HD), F32)],
        [
            pltpu.VMEM((rows, span, 2 * HD), BF16),
            pltpu.VMEM((rows, group_heads * HD), BF16),
            pltpu.SMEM((rows,), jnp.int32),
            pltpu.VMEM((top, rows), jnp.int32),
            pltpu.VMEM((top, rows), F32),
            pltpu.VMEM((many, HD), F32),
            pltpu.VMEM((many, span), F32),
            pltpu.VMEM((many + group_heads, HD), F32),
            pltpu.VMEM((many + group_heads, HD), F32),
            pltpu.VMEM((many + group_heads, HD), F32),
            pltpu.SemaphoreType.DMA((3 + len(CUTS),)),
        ],
        far=range(5),
        limit=16,
        name="attention",
    )
    own, *rest = results[:kv_parts]
    gate_lanes = results[kv_parts]
    out_weight, resid, gain, token = fetched(
        gate_lanes, out_weight, resid, norm_gain.reshape(1, width)
    )
    came = [swapped(rest[mask - 1], "tp", mask) for mask in range(1, kv_parts)]
    heads, away = call(
        functools.partial(project_kernel, (kv_parts, per_member, half)),
        [token, out_weight, own, *came],
        [((rows, per_member * HD), BF16), ((rows, half), BF16)],
        name="project",
    )
    away = swapped(away, "side", 1)
    kept = call(
        functools.partial(part_kernel, True), [heads, out_weight], [((rows, half), F32)], name="kept"
    )[0]
    outgoing = call(add_kernel, [kept, away], [((rows, half), BF16)], name="pair")[0]
    w_gate_up, token = fetched(outgoing, w_gate_up)
    parts = [crossed(outgoing, 0, mask) for mask in range(tp)]
    middle, packet = call(
        functools.partial(middle_kernel, half),
        [token, resid, gate_lanes, *parts],
        [((rows, half), BF16), ((half // HD * rows + 2 * grp, HD), BF16)],
        name="middle",
    )
    packets = [crossed(packet, mask) for mask in [*range(1, grp), 0]]
    packets = [packets[-1], *packets[:-1]]
    near_packets = [packet] + [swapped(p, "side", 1) for p in packets[1:]]
    total = grp * rows
    tile = 256
    hidden, square, gate = call(
        functools.partial(first_half_kernel, tile, rows, half),
        [gain, w_gate_up, *packets],
        [((total, 2 * inner), F32), ((total, HD), F32), ((total, HD), F32)],
        name="first_half",
    )
    act, sent = call(
        functools.partial(second_half_kernel, tile, rows, half),
        [gain, w_gate_up, hidden, square, gate, w_down, *near_packets],
        [((total, inner), BF16), ((total, half), BF16)],
        name="second_half",
    )
    back = swapped(sent, "side", 1)
    mine = call(
        functools.partial(keep_kernel, tile),
        [act, gate, w_down],
        [((total, half), F32)],
        name="keep",
    )[0]
    sends = call(
        functools.partial(fold_kernel, rows),
        [mine, back],
        [((rows, half), BF16)] * grp,
        name="fold",
    )
    came = [crossed(sends[mask], mask) for mask in reversed(range(grp))]
    sends = call(
        functools.partial(split_kernel, grp),
        came,
        [((rows, piece), BF16)] * tp,
        name="split",
    )
    came = [crossed(sends[mask], 0, mask) for mask in reversed(range(tp))]
    ins = [middle, *came]
    return pl.pallas_call(
        final_kernel,
        out_shape=jax.ShapeDtypeStruct((rows, piece), BF16),
        in_specs=[VMEM_SPEC] * len(ins),
        out_specs=VMEM_SPEC,
        name="final",
    )(*map(near, ins))


def solution(mesh):
    in_specs = (
        P("grp", "side"),
        P("grp", ("side", "tp"), None, None),
        P("grp"),
        P(("side", "tp"), None),
        P("grp", None),
        P(),
        P("grp", None),
        P("grp", None),
        P(("side", "grp", "tp"), None, None),
        P(("side", "grp", "tp"), None, None),
    )
    out_specs = P("grp", ("side", "tp"))
    return jax.shard_map(body, mesh=mesh, in_specs=in_specs, out_specs=out_specs, check_vma=False)
```
